128 devices in a mesh: row: 16 (over x, z), col: 8 (over y, core).
Axes of the slice: x: 4, y: 4, z: 4, core: 2. Of those that a mesh axis runs over, the one named last changes fastest.
Arguments:
- positions: float32 [3, 32768], P(None, ('row', 'col')), may hold values from 0 to 4
- primal: bfloat16 [32768, 32], P(('row', 'col')), may hold values from -0.59765625 to 0.59765625
- adjoint: bfloat16 [32768, 32], P(('row', 'col')), may hold values from -0.59765625 to 0.59765625
- support: int32 [4, 32768], P(None, ('row', 'col')), may hold values from 0 to 2047
- basis: float32 [4, 32768], P(None, ('row', 'col')), may hold values from 0.1 to 1
Outputs:
- cp_gradient: float32 [3, 2048], P(None, ('row', 'col'))
The draws below stay inside these ranges and needn't reach their ends.
All inputs are finite; a program needn't handle non-finite values.
Results may differ from the reference program's by a relative error of at most 0.0011.
Values may be sent and summed in bfloat16 or wider, within the bound.
A program may use at most 64 MiB of HBM per device.

```python
import math
import jax
import jax.numpy as jnp
from jax import lax

STR = 32
CP = 2048
SUPP = 4
N = 32768


def place_ends(drawn, rng, least, largest):
    index_at = [jax.random.randint(jax.random.fold_in(rng, axis), (), 0, length) for axis, length in enumerate(drawn.shape)]
    main_axis = drawn.shape.index(max(drawn.shape))
    neighbour = index_at[:main_axis] + [(index_at[main_axis] + 1) % drawn.shape[main_axis]] + index_at[main_axis + 1:]
    return drawn.at[tuple(index_at)].set(least).at[tuple(neighbour)].set(largest)


def shard_levels(own_key, shape, split, least, high):
    factor_of, own = 1.0, jax.random.fold_in(own_key, 6)
    for dim, shards_of in split:
        steps = jnp.exp(jax.random.uniform(jax.random.fold_in(own, dim), (shards_of,), jnp.float32, least / len(split), high / len(split)))
        factor_of = factor_of * jnp.repeat(steps, shape[dim] // shards_of).reshape([-1 if axis == dim else 1 for axis in range(len(shape))])
    return factor_of


def centred(key, extent, spread, limit, cuts=(), held_as=jnp.bfloat16):
    gain = shard_levels(key, extent, cuts, -0.22, 0.18) if cuts else 1.0
    drawn = jax.random.normal(key, extent, jnp.float32) * spread * gain
    return jnp.minimum(jnp.maximum(drawn, -limit), limit).astype(held_as)


def setup_inputs(seed: int = 0) -> dict:
    seeds = jax.random.split(jax.random.key(seed), 6)
    return {
        "positions": jnp.clip(4.0 * jax.random.uniform(seeds[0], (3, N), jnp.float32) ** shard_levels(seeds[0], (3, N), ((1, 128),), -0.2, 0.2), 0.0, 4.0),
        "primal": centred(seeds[1], (N, STR), 0.1, 0.59765625, ((0, 128),)),
        "adjoint": centred(seeds[2], (N, STR), 0.1, 0.59765625, ((0, 128),)),
        "support": place_ends(jax.random.randint(seeds[3], (SUPP, N), 0, CP), jax.random.fold_in(seeds[3], 1), 0, CP - 1).astype(jnp.int32),
        "basis": jnp.clip(jnp.exp(math.log(1.0) - 2.3025851 * jax.random.uniform(seeds[4], (SUPP, N), jnp.float32) ** shard_levels(seeds[4], (SUPP, N), ((1, 128),), -0.2, 0.2)), 0.1, 1.0),
    }


core_sq = 0.01

def pair_terms(xt, xs, weights):
    dist = core_sq + (xt[0][:, None] - xs[0][None, :]) ** 2
    dist = dist + (xt[1][:, None] - xs[1][None, :]) ** 2
    dist = dist + (xt[2][:, None] - xs[2][None, :]) ** 2
    inverse = lax.rsqrt(dist)
    paired = weights * inverse * inverse * inverse
    aug_t = jnp.concatenate([xt, jnp.ones((1, xt.shape[1]), xt.dtype)], 0)
    aug_s = jnp.concatenate([xs, jnp.ones((1, xs.shape[1]), xs.dtype)], 0)
    upper = jnp.dot(aug_t, paired, precision=lax.Precision.HIGHEST)
    lower = lax.dot_general(aug_s, paired, (((1,), (1,)), ((), ())), precision=lax.Precision.HIGHEST)
    source_part = upper[:3] - xs * upper[3:4]
    target_part = lower[:3] - xt * lower[3:4]
    return (source_part, target_part)

def to_points(total, grad, sup, bas):
    for k in range(sup.shape[0]):
        total = total.at[:, sup[k]].add(bas[k][None, :] * grad)
    return total

def reference(positions, primal, adjoint, support, basis):
    count = positions.shape[1]
    blk = min(512, count)

    def block(k, carry):
        src, tgt = carry
        start = (k * blk).astype(jnp.int32)
        xt = lax.dynamic_slice_in_dim(positions, start, blk, 1)
        lt = lax.dynamic_slice_in_dim(adjoint, start, blk, 0)
        weights = lax.dot_general(lt, primal, (((1,), (1,)), ((), ())), preferred_element_type=jnp.float32)
        part_src, part_tgt = pair_terms(xt, positions, weights)
        tgt = lax.dynamic_update_slice_in_dim(tgt, part_tgt, start, 1)
        return (src + part_src, tgt)
    zero = jnp.zeros(positions.shape, positions.dtype)
    src, tgt = lax.fori_loop(0, count // blk, block, (zero, zero))
    total = jnp.zeros((3, CP), positions.dtype)
    return to_points(total, src + tgt, support, basis)
```

```python
import numpy as np
import jax
import jax.numpy as jnp
from jax import lax
from jax.experimental import pallas as pl
from jax.experimental.pallas import tpu as pltpu
from jax.sharding import PartitionSpec as P

f32, bf16 = jnp.float32, jnp.bfloat16
MESH = pl.DeviceIdType.MESH
NT = (((1,), (1,)), ((), ()))
TN = (((0,), (0,)), ((), ()))

STR, CP, CORE_SQ, SHIFT = 32, 2048, 0.01, 2.0
PB = 256
NCOL, NROW, SIDE = 8, 16, 4
FULL = ((1, 0), (0, 1), (1, 1), (3, 1), (3, 2), (2, 3))
HALF = ((2, 0), (0, 2), (2, 2))
OFFS = FULL + HALF
ROWS = 96
CHUNK = 32


def selectors():
    left = np.zeros((80, 512), np.float32)
    for s in range(STR):
        left[STR + s, s] = 1.0
        left[s, STR + s] = 1.0
    h, m, l, n, one = 64, 67, 70, 73, 76
    for part, rows in enumerate((h, m, l)):
        base = 64 + 16 * part
        for c in range(3):
            for slot in (c, 3 + c, 6 + c):
                left[rows + c, base + slot] = -2.0
        left[n + part, base + 12] = 1.0
    for k in range(3):
        left[one, 64 + 9 + k] = 1.0
    for c in range(3):
        for rows in (h, m, l):
            left[rows + c, 128 + 128 * c : 256 + 128 * c] = 1.0
    return left


def split3(x):
    h = x.astype(bf16)
    rest = x - h.astype(f32)
    m = rest.astype(bf16)
    return h, m, (rest - m.astype(f32)).astype(bf16)


def kernel(
    pos_ref, prim_ref, adj_ref, sup_ref, bas_ref, sel_ref, eye_ref, out_ref,
    ta, tb, aw, ad, xa, acc_a, acc_b, grad_a, s1, r1, s2, r2,
    send_a, recv_a, send_b, recv_b, send_1, recv_1, send_2, recv_2,
):
    row, col = lax.axis_index("row"), lax.axis_index("col")
    rx, rz = row // SIDE, row % SIDE

    def at_row(off):
        return ((rx + off[0]) % SIDE) * SIDE + (rz + off[1]) % SIDE

    def at_col(d):
        return (col + d) % NCOL

    barrier = pltpu.get_barrier_semaphore()
    for d in range(1, NCOL):
        pl.semaphore_signal(barrier, inc=1, device_id=(row, at_col(d)), device_id_type=MESH)
    for k in range(1, NROW):
        other = at_row((k // SIDE, k % SIDE))
        pl.semaphore_signal(barrier, inc=1, device_id=(other, col), device_id_type=MESH)

    eye = eye_ref[...]
    ta[0, 0:32] = lax.dot_general(eye, adj_ref[...], NT, preferred_element_type=f32).astype(bf16)
    ta[0, 32:64] = lax.dot_general(eye, prim_ref[...], NT, preferred_element_type=f32).astype(bf16)
    u = pos_ref[...] - SHIFT
    n = jnp.sum(u * u, axis=0, keepdims=True) + 0.5 * CORE_SQ
    uh, um, ul = split3(u)
    nh, nm, nl = split3(n)
    feats = [p.astype(f32) for p in (uh, um, ul, nh, nm, nl)]
    feats.append(jnp.ones((1, PB), f32))
    feats.append(jnp.zeros((3, PB), f32))
    ta[0, 64:80] = jnp.concatenate(feats, axis=0).astype(bf16)
    sup = sup_ref[...]
    bas = bas_ref[...]
    bh = bas.astype(bf16).astype(f32)
    bm = bas - bh
    ta[0, 80:96] = jnp.concatenate(
        [(sup // 128).astype(f32), (sup % 128).astype(f32), bh, bm], axis=0
    ).astype(bf16)

    pl.semaphore_wait(barrier, NCOL - 1 + NROW - 1)

    def copy_a(d):
        return pltpu.make_async_remote_copy(
            src_ref=ta.at[0], dst_ref=ta.at[d], send_sem=send_a.at[d - 1], recv_sem=recv_a.at[d - 1],
            device_id=(row, at_col(-d)), device_id_type=MESH,
        )

    def copy_b(k):
        off = OFFS[k]
        return pltpu.make_async_remote_copy(
            src_ref=ta.at[0], dst_ref=tb.at[k], send_sem=send_b.at[k], recv_sem=recv_b.at[k],
            device_id=(at_row((-off[0], -off[1])), col), device_id_type=MESH,
        )

    for d in range(1, 5):
        copy_a(d).start()
    for d in range(5, NCOL):
        copy_a(d).start()
    for k in range(len(OFFS)):
        copy_b(k).start()

    acc_a[...] = jnp.zeros_like(acc_a)

    def prepare(d):
        left = lax.dot_general(ta[d, 0:80], sel_ref[...], TN, preferred_element_type=f32)
        aw[d] = left[:, 0:64].astype(bf16)
        ad[d] = left[:, 64:112].astype(bf16)
        for c in range(3):
            xa[d, c] = left[:, 128 * (c + 1) : 128 * (c + 2)]

    def pairs(right, slots, store, half=()):
        parts = right[64:80]
        rd = jnp.concatenate([parts, parts, parts], axis=0)
        accs = [None] * 4
        for i, slot in enumerate(slots):
            rw = right[0:64]
            if i in half:
                rw = rw * jnp.asarray(0.5, bf16)
            w = jnp.dot(aw[slot], rw, preferred_element_type=f32)
            d = jnp.dot(ad[slot], rd, preferred_element_type=f32)
            his, los = [], []
            for q in range(PB // CHUNK):
                rs = slice(q * CHUNK, (q + 1) * CHUNK)
                inv = lax.rsqrt(d[rs])
                s = w[rs] * inv * (inv * inv)
                for c in range(4):
                    if c < 3:
                        x = xa[slot, c, rs]
                        t = s * jnp.concatenate([x, x], axis=1)
                    else:
                        t = s
                    t = jnp.sum(t.reshape(CHUNK // 8, 8, PB), axis=0)
                    accs[c] = t if accs[c] is None else accs[c] + t
                hi = s.astype(bf16)
                his.append(hi)
                los.append((s - hi.astype(f32)).astype(bf16))
            hi, lo = jnp.concatenate(his, axis=0), jnp.concatenate(los, axis=0)
            acc_a[slot] += lax.dot_general(parts, hi, NT, preferred_element_type=f32) + lax.dot_general(
                parts, lo, NT, preferred_element_type=f32
            )
        for c in range(4):
            acc_b[store, c] = accs[c]

    prepare(0)
    for d in range(1, 5):
        copy_a(d).wait_recv()
        prepare(d)
    pairs(ta.at[0], range(5), len(OFFS), half=(0, 4))
    for d in range(5, NCOL):
        copy_a(d).wait_recv()
        prepare(d)

    def full(k, _):
        pltpu.make_async_remote_copy(
            src_ref=ta.at[0], dst_ref=tb.at[k], send_sem=send_b.at[k], recv_sem=recv_b.at[k],
            device_id=(row, at_col(1)), device_id_type=MESH,
        ).wait_recv()
        pairs(tb.at[k], range(NCOL), k)
        return 0

    lax.fori_loop(0, len(FULL), full, 0)
    for k in range(len(FULL), len(OFFS)):
        copy_b(k).wait_recv()
        later = (at_row(OFFS[k]) < row).astype(jnp.int32)
        pairs(tb.at[k], [later + i for i in range(4)], k)

    def coords(bundle):
        p = bundle[64:80].astype(f32)
        return p[0:3] + p[3:6] + p[6:9]

    def from_b(k, bundle):
        sums = [jnp.sum(acc_b[k, c], axis=0, keepdims=True) for c in range(4)]
        return jnp.concatenate(sums[:3], axis=0) - coords(bundle) * sums[3]

    def from_a(d):
        t = acc_a[d]
        return t[0:3] + t[3:6] + t[6:9] - coords(ta.at[d]) * t[12:13]

    rows16 = lax.broadcasted_iota(jnp.int32, (16, PB), 0).astype(f32)
    rows128 = lax.broadcasted_iota(jnp.int32, (128, PB), 0).astype(f32)

    def scatter(total, grad, bundle):
        data = bundle[80:96].astype(f32)
        for k in range(4):
            val = grad * (data[8 + k : 9 + k] + data[12 + k : 13 + k])
            here = rows16 == data[k : k + 1]
            left = jnp.concatenate([jnp.where(here, val[c : c + 1], 0.0) for c in range(3)], axis=0)
            hi = left.astype(bf16)
            lo = (left - hi.astype(f32)).astype(bf16)
            hot = jnp.where(rows128 == data[4 + k : 5 + k], 1.0, 0.0).astype(bf16)
            total = total + lax.dot_general(hi, hot, NT, preferred_element_type=f32)
            total = total + lax.dot_general(lo, hot, NT, preferred_element_type=f32)
        return total

    total = jnp.zeros((48, 128), f32)
    total = scatter(total, from_a(0) + from_b(len(OFFS), ta.at[0]), ta.at[0])
    total = lax.fori_loop(1, NCOL, lambda d, t: scatter(t, from_a(d), ta.at[d]), total)
    total = lax.fori_loop(0, len(OFFS), lambda k, t: scatter(t, from_b(k, tb.at[k]), tb.at[k]), total)

    zeros = jnp.zeros((5, 128), f32)
    for q in range(NROW):
        s1[q] = jnp.concatenate([total[q : q + 1], total[16 + q : 17 + q], total[32 + q : 33 + q], zeros], axis=0)

    def copy_1(k):
        other = at_row((k // SIDE, k % SIDE))
        return pltpu.make_async_remote_copy(
            src_ref=s1.at[other], dst_ref=r1.at[k - 1], send_sem=send_1.at[k - 1], recv_sem=recv_1.at[k - 1],
            device_id=(other, col), device_id_type=MESH,
        )

    def copy_2(d):
        return pltpu.make_async_remote_copy(
            src_ref=s2, dst_ref=r2.at[d - 1], send_sem=send_2.at[d - 1], recv_sem=recv_2.at[d - 1],
            device_id=(row, at_col(d)), device_id_type=MESH,
        )

    for k in range(1, NROW):
        copy_1(k).start()
    mine = s1[row]
    for k in range(1, NROW):
        copy_1(k).wait_recv()
        mine = mine + r1[k - 1]
    s2[...] = mine
    for d in range(1, NCOL):
        copy_2(d).start()
    for d in range(1, NCOL):
        copy_2(d).wait_recv()
        mine = mine + r2[d - 1]
    mine = pltpu.roll(mine, (128 - 16 * col) % 128, 1)
    out_ref[...] = mine[0:3, 0:16]

    for d in range(1, NCOL):
        copy_a(d).wait_send()
        copy_2(d).wait_send()
    for k in range(len(OFFS)):
        copy_b(k).wait_send()
    for k in range(1, NROW):
        copy_1(k).wait_send()


def shards(positions, primal, adjoint, support, basis):
    sel = jnp.asarray(selectors(), bf16)
    eye = jnp.asarray(np.eye(STR, dtype=np.float32), bf16)
    vmem = pl.BlockSpec(memory_space=pltpu.VMEM)
    dma = pltpu.SemaphoreType.DMA
    nb = len(OFFS)
    return pl.pallas_call(
        kernel,
        out_shape=jax.ShapeDtypeStruct((3, 16), f32),
        in_specs=[vmem] * 7,
        out_specs=vmem,
        scratch_shapes=[
            pltpu.VMEM((NCOL, ROWS, PB), bf16),
            pltpu.VMEM((nb, ROWS, PB), bf16),
            pltpu.VMEM((NCOL, PB, 64), bf16),
            pltpu.VMEM((NCOL, PB, 48), bf16),
            pltpu.VMEM((NCOL, 3, PB, 128), f32),
            pltpu.VMEM((NCOL, 16, PB), f32),
            pltpu.VMEM((nb + 1, 4, 8, PB), f32),
            pltpu.VMEM((8, 128), f32),
            pltpu.VMEM((NROW, 8, 128), f32),
            pltpu.VMEM((NROW - 1, 8, 128), f32),
            pltpu.VMEM((8, 128), f32),
            pltpu.VMEM((NCOL - 1, 8, 128), f32),
            dma((NCOL - 1,)), dma((NCOL - 1,)), dma((nb,)), dma((nb,)),
            dma((NROW - 1,)), dma((NROW - 1,)), dma((NCOL - 1,)), dma((NCOL - 1,)),
        ],
        compiler_params=pltpu.CompilerParams(
            collective_id=0, has_side_effects=True, vmem_limit_bytes=48 * 2**20
        ),
    )(positions, primal, adjoint, support, basis, sel, eye)


def solution(mesh):
    in_specs = (
        P(None, ("row", "col")),
        P(("row", "col"), None),
        P(("row", "col"), None),
        P(None, ("row", "col")),
        P(None, ("row", "col")),
    )
    out_specs = P(None, ("row", "col"))
    return jax.shard_map(shards, mesh=mesh, in_specs=in_specs, out_specs=out_specs, check_vma=False)
```

```python
import numpy as np
import jax
import jax.numpy as jnp
from jax import lax
from jax.experimental import pallas as pl
from jax.experimental.pallas import tpu as pltpu
from jax.sharding import PartitionSpec as P

f32, bf16 = jnp.float32, jnp.bfloat16
MESH = pl.DeviceIdType.MESH
NT = (((1,), (1,)), ((), ()))
TN = (((0,), (0,)), ((), ()))

STR, CP, CORE_SQ, SHIFT = 32, 2048, 0.01, 2.0
PB = 256
NCOL, NROW, SIDE = 8, 16, 4
FULL = ((1, 0), (0, 1), (1, 1), (3, 1), (3, 2), (2, 3))
HALF = ((2, 0), (0, 2), (2, 2))
OFFS = FULL + HALF
ROWS = 96
CHUNK = 32


def selectors():
    left = np.zeros((80, 512), np.float32)
    for s in range(STR):
        left[STR + s, s] = 1.0
        left[s, STR + s] = 1.0
    h, m, l, n, one = 64, 67, 70, 73, 76
    for part, rows in enumerate((h, m, l)):
        base = 64 + 16 * part
        for c in range(3):
            for slot in (c, 3 + c, 6 + c):
                left[rows + c, base + slot] = -2.0
        left[n + part, base + 12] = 1.0
    for k in range(3):
        left[one, 64 + 9 + k] = 1.0
    for c in range(3):
        for rows in (h, m, l):
            left[rows + c, 128 + 128 * c : 256 + 128 * c] = 1.0
    return left


def split3(x):
    h = x.astype(bf16)
    rest = x - h.astype(f32)
    m = rest.astype(bf16)
    return h, m, (rest - m.astype(f32)).astype(bf16)


def kernel(
    pos_hbm, prim_hbm, adj_hbm, sup_hbm, bas_hbm, sel_hbm, out_ref,
    pos_v, sup_v, bas_v, sel_v, ta, tb, aw, ad, xa, acc_a, acc_b, s1, r1, s2, r2,
    load, send_a, recv_a, send_b, recv_b, send_1, recv_1, send_2, recv_2,
):
    row, col = lax.axis_index("row"), lax.axis_index("col")
    rx, rz, cy, core = row // SIDE, row % SIDE, col // 2, col % 2

    def at_row(off):
        return ((rx + off[0]) % SIDE) * SIDE + (rz + off[1]) % SIDE

    def at_col(slot, sign=1):
        return ((cy + sign * (slot // 2)) % SIDE) * 2 + (core + slot) % 2

    barrier = pltpu.get_barrier_semaphore()
    for slot in range(1, NCOL):
        pl.semaphore_signal(barrier, inc=1, device_id=(row, at_col(slot)), device_id_type=MESH)
    for k in range(1, NROW):
        other = at_row((k // SIDE, k % SIDE))
        pl.semaphore_signal(barrier, inc=1, device_id=(other, col), device_id_type=MESH)

    loads = [
        pltpu.make_async_copy(src, dst, load.at[i])
        for i, (src, dst) in enumerate((
            (pos_hbm, pos_v), (sup_hbm, sup_v), (bas_hbm, bas_v), (sel_hbm, sel_v),
            (adj_hbm, ta.at[0, 0:32]), (prim_hbm, ta.at[0, 32:64]),
        ))
    ]
    for copy in loads:
        copy.start()
    acc_a[...] = jnp.zeros_like(acc_a)
    for copy in loads[:3]:
        copy.wait()
    u = pos_v[...] - SHIFT
    n = jnp.sum(u * u, axis=0, keepdims=True) + 0.5 * CORE_SQ
    uh, um, ul = split3(u)
    nh, nm, nl = split3(n)
    feats = [p.astype(f32) for p in (uh, um, ul, nh, nm, nl)]
    feats.append(jnp.ones((1, PB), f32))
    feats.append(jnp.zeros((3, PB), f32))
    sup = sup_v[...]
    bas = bas_v[...]
    bh = bas.astype(bf16).astype(f32)
    feats += [(sup // 16).astype(f32), (sup % 16).astype(f32), bh, bas - bh]
    ta[0, 64:96] = jnp.concatenate(feats, axis=0).astype(bf16)
    for copy in loads[3:]:
        copy.wait()

    pl.semaphore_wait(barrier, NCOL - 1 + NROW - 1)

    def copy_a(slot):
        src = 0 if slot % 2 == 0 or slot == 1 else slot - 1
        to = at_col(slot, -1) if src == 0 else at_col(1)
        return pltpu.make_async_remote_copy(
            src_ref=ta.at[src], dst_ref=ta.at[slot], send_sem=send_a.at[slot - 1], recv_sem=recv_a.at[slot - 1],
            device_id=(row, to), device_id_type=MESH,
        )

    def copy_b(k):
        off = OFFS[k]
        return pltpu.make_async_remote_copy(
            src_ref=ta.at[0], dst_ref=tb.at[k], send_sem=send_b.at[k], recv_sem=recv_b.at[k],
            device_id=(at_row((-off[0], -off[1])), col), device_id_type=MESH,
        )

    for slot in (1, 2, 6, 4):
        copy_a(slot).start()
    for k in (0, 1):
        copy_b(k).start()

    def prepare(slot):
        left = lax.dot_general(ta[slot, 0:80], sel_v[...], TN, preferred_element_type=f32)
        aw[slot] = left[:, 0:64].astype(bf16)
        ad[slot] = left[:, 64:112].astype(bf16)
        for c in range(3):
            xa[slot, c] = left[:, 128 * (c + 1) : 128 * (c + 2)]

    def pairs(right, slots, store, half=(), first=True):
        parts = right[64:80]
        rd = jnp.concatenate([parts, parts, parts], axis=0)
        accs = [None] * 4
        for i, slot in enumerate(slots):
            rw = right[0:64]
            if i in half:
                rw = rw * jnp.asarray(0.5, bf16)
            w = jnp.dot(aw[slot], rw, preferred_element_type=f32)
            d = jnp.dot(ad[slot], rd, preferred_element_type=f32)
            his, los = [], []
            for q in range(PB // CHUNK):
                rs = slice(q * CHUNK, (q + 1) * CHUNK)
                inv = lax.rsqrt(d[rs])
                s = w[rs] * inv * (inv * inv)
                for c in range(4):
                    if c < 3:
                        x = xa[slot, c, rs]
                        t = s * jnp.concatenate([x, x], axis=1)
                    else:
                        t = s
                    t = jnp.sum(t.reshape(CHUNK // 8, 8, PB), axis=0)
                    accs[c] = t if accs[c] is None else accs[c] + t
                hi = s.astype(bf16)
                his.append(hi)
                los.append((s - hi.astype(f32)).astype(bf16))
            hi, lo = jnp.concatenate(his, axis=0), jnp.concatenate(los, axis=0)
            acc_a[slot] += lax.dot_general(parts, hi, NT, preferred_element_type=f32) + lax.dot_general(
                parts, lo, NT, preferred_element_type=f32
            )
        for c in range(4):
            acc_b[store, c] = accs[c] if first else acc_b[store, c] + accs[c]

    nb = len(OFFS)
    own = ta.at[0]
    prepare(0)
    pairs(own, [0], nb, half=(0,))
    copy_a(1).wait_recv()
    prepare(1)
    pairs(own, [1], nb, half=(0,), first=False)
    for slot in (2, 6, 4):
        copy_a(slot).wait_recv()
        copy_a(slot + 1).start()
    for k in (2, 3, 4):
        copy_b(k).start()
    prepare(2)
    prepare(4)
    prepare(6)
    pairs(own, [2, 4], nb, half=(1,), first=False)
    for k in range(5, nb):
        copy_b(k).start()
    for slot in (3, 7, 5):
        copy_a(slot).wait_recv()
        prepare(slot)
    pairs(own, [3, 5], nb, half=(1,), first=False)

    def arrived(k):
        pltpu.make_async_remote_copy(
            src_ref=ta.at[0], dst_ref=tb.at[k], send_sem=send_b.at[k], recv_sem=recv_b.at[k],
            device_id=(row, at_col(1)), device_id_type=MESH,
        ).wait_recv()

    def full(k, _):
        arrived(k)
        pairs(tb.at[k], range(NCOL), k)
        return 0

    def halved(k, _):
        arrived(k)
        i = k - len(FULL)
        first = 2 * (at_row((2 * ((i + 1) % 2), 2 * ((i + 1) // 2))) < row).astype(jnp.int32)
        pairs(tb.at[k], [first + j for j in range(4)], k)
        return 0

    lax.fori_loop(0, len(FULL), full, 0)
    lax.fori_loop(len(FULL), nb, halved, 0)

    def coords(bundle):
        p = bundle[64:80].astype(f32)
        return p[0:3] + p[3:6] + p[6:9]

    def from_b(k, bundle):
        sums = [jnp.sum(acc_b[k, c], axis=0, keepdims=True) for c in range(4)]
        return jnp.concatenate(sums[:3], axis=0) - coords(bundle) * sums[3]

    def from_a(slot):
        t = acc_a[slot]
        return t[0:3] + t[3:6] + t[6:9] - coords(ta.at[slot]) * t[12:13]

    rows16 = lax.broadcasted_iota(jnp.int32, (16, PB), 0).astype(f32).astype(bf16)
    rows128 = lax.broadcasted_iota(jnp.int32, (128, PB), 0).astype(f32).astype(bf16)
    zero, unit = jnp.zeros((), bf16), jnp.ones((), bf16)

    def scatter(total, grad, bundle):
        data = bundle[80:96]
        basis = data[8:12].astype(f32) + data[12:16].astype(f32)
        lefts, rights = [], []
        for k in range(4):
            val = grad * basis[k : k + 1]
            hi = val.astype(bf16)
            lo = (val - hi.astype(f32)).astype(bf16)
            here = rows16 == data[4 + k : 5 + k]
            rights.append(
                jnp.concatenate([jnp.where(here, p[c : c + 1], zero) for p in (hi, lo) for c in range(3)], axis=0)
            )
            lefts.append(jnp.where(rows128 == data[k : k + 1], unit, zero))
        left, right = jnp.concatenate(lefts, axis=1), jnp.concatenate(rights, axis=1)
        return total + lax.dot_general(left, right, NT, preferred_element_type=f32)

    total = jnp.zeros((128, 96), f32)
    total = scatter(total, from_a(0) + from_b(nb, own), own)
    total = lax.fori_loop(1, NCOL, lambda d, t: scatter(t, from_a(d), ta.at[d]), total)
    total = lax.fori_loop(0, nb, lambda k, t: scatter(t, from_b(k, tb.at[k]), tb.at[k]), total)
    total = jnp.concatenate([total[:, 0:48] + total[:, 48:96], jnp.zeros((128, 80), f32)], axis=1)

    s1[...] = total.reshape(NROW, NCOL, 128)

    def copy_1(k):
        other = at_row((k // SIDE, k % SIDE))
        return pltpu.make_async_remote_copy(
            src_ref=s1.at[other], dst_ref=r1.at[k - 1], send_sem=send_1.at[k - 1], recv_sem=recv_1.at[k - 1],
            device_id=(other, col), device_id_type=MESH,
        )

    def copy_2(slot):
        return pltpu.make_async_remote_copy(
            src_ref=s2, dst_ref=r2.at[slot - 1], send_sem=send_2.at[slot - 1], recv_sem=recv_2.at[slot - 1],
            device_id=(row, at_col(slot)), device_id_type=MESH,
        )

    for k in range(1, NROW):
        copy_1(k).start()
    mine = s1[row]
    for k in range(1, NROW):
        copy_1(k).wait_recv()
        mine = mine + r1[k - 1]
    s2[...] = mine
    for slot in range(1, NCOL):
        copy_2(slot).start()
    for slot in range(1, NCOL):
        copy_2(slot).wait_recv()
        mine = mine + r2[slot - 1]
    here = lax.broadcasted_iota(jnp.int32, (NCOL, 128), 0) == col
    line = jnp.sum(jnp.where(here, mine, 0.0), axis=0, keepdims=True)
    out_ref[...] = jnp.concatenate([line[:, 16 * c : 16 * (c + 1)] for c in range(3)], axis=0)

    for slot in range(1, NCOL):
        copy_a(slot).wait_send()
        copy_2(slot).wait_send()
    for k in range(nb):
        copy_b(k).wait_send()
    for k in range(1, NROW):
        copy_1(k).wait_send()


def shards(positions, primal, adjoint, support, basis):
    sel = jnp.asarray(selectors(), bf16)
    vmem = pl.BlockSpec(memory_space=pltpu.VMEM)
    hbm = pl.BlockSpec(memory_space=pltpu.HBM)
    dma = pltpu.SemaphoreType.DMA
    nb = len(OFFS)
    return pl.pallas_call(
        kernel,
        out_shape=jax.ShapeDtypeStruct((3, 16), f32),
        in_specs=[hbm] * 6,
        out_specs=vmem,
        scratch_shapes=[
            pltpu.VMEM((3, PB), f32),
            pltpu.VMEM((4, PB), jnp.int32),
            pltpu.VMEM((4, PB), f32),
            pltpu.VMEM((80, 512), bf16),
            pltpu.VMEM((NCOL, ROWS, PB), bf16),
            pltpu.VMEM((nb, ROWS, PB), bf16),
            pltpu.VMEM((NCOL, PB, 64), bf16),
            pltpu.VMEM((NCOL, PB, 48), bf16),
            pltpu.VMEM((NCOL, 3, PB, 128), f32),
            pltpu.VMEM((NCOL, 16, PB), f32),
            pltpu.VMEM((nb + 1, 4, 8, PB), f32),
            pltpu.VMEM((NROW, 8, 128), f32),
            pltpu.VMEM((NROW - 1, 8, 128), f32),
            pltpu.VMEM((8, 128), f32),
            pltpu.VMEM((NCOL - 1, 8, 128), f32),
            dma((6,)), dma((NCOL - 1,)), dma((NCOL - 1,)), dma((nb,)), dma((nb,)),
            dma((NROW - 1,)), dma((NROW - 1,)), dma((NCOL - 1,)), dma((NCOL - 1,)),
        ],
        compiler_params=pltpu.CompilerParams(
            collective_id=0, has_side_effects=True, vmem_limit_bytes=48 * 2**20
        ),
    )(positions, primal.T, adjoint.T, support, basis, sel)


def solution(mesh):
    in_specs = (
        P(None, ("row", "col")),
        P(("row", "col"), None),
        P(("row", "col"), None),
        P(None, ("row", "col")),
        P(None, ("row", "col")),
    )
    out_specs = P(None, ("row", "col"))
    return jax.shard_map(shards, mesh=mesh, in_specs=in_specs, out_specs=out_specs, check_vma=False)
```

```python
import jax
import jax.numpy as jnp
from jax import lax
from jax.experimental import pallas as pl
from jax.experimental.pallas import tpu as pltpu
from jax.sharding import PartitionSpec as P

f32, bf16 = jnp.float32, jnp.bfloat16
MESH = pl.DeviceIdType.MESH
NT = (((1,), (1,)), ((), ()))
TN = (((0,), (0,)), ((), ()))

STR, CP, CORE_SQ, SHIFT = 32, 2048, 0.01, 2.0
PB = 256
NCOL, NROW, SIDE = 8, 16, 4
FULL = ((1, 0), (0, 1), (1, 1), (3, 1), (3, 2), (2, 3))
HALF = ((2, 0), (0, 2), (2, 2))
OFFS = FULL + HALF
FAR = sorted(
    ((x, y, z) for x in range(SIDE) for y in range(SIDE) for z in range(SIDE) if x or y or z),
    key=lambda o: -sum(min(v, SIDE - v) for v in o),
)
ROWS = 96
CHUNK = 32


def selectors():
    r = lax.broadcasted_iota(jnp.int32, (80, 512), 0)
    c = lax.broadcasted_iota(jnp.int32, (80, 512), 1)
    weights = (c < 2 * STR) & (r < 2 * STR) & (r == (c + STR) % (2 * STR))
    part, slot = (c - 64) // 16, c % 16
    r3, slot3 = (r - 64) % 3, slot % 3
    distance = (c >= 64) & (c < 112)
    cross = distance & (slot < 9) & (r >= 64) & (r < 73) & ((r - 64) // 3 == part) & (r3 == slot3)
    norm = distance & (slot == 12) & (r == 73 + part)
    norm = norm | (distance & (part == 0) & (slot >= 9) & (slot < 12) & (r == 76))
    spread = (c >= 128) & (r >= 64) & (r < 73) & (r3 == (c - 128) // 128)
    return jnp.where(cross, -2.0, jnp.where(weights | norm | spread, 1.0, 0.0)).astype(bf16)


def split3(x):
    h = x.astype(bf16)
    rest = x - h.astype(f32)
    m = rest.astype(bf16)
    return h, m, (rest - m.astype(f32)).astype(bf16)


def kernel(
    pos_hbm, prim_hbm, adj_hbm, sup_hbm, bas_hbm, out_ref,
    pos_v, sup_v, bas_v, sel_v, ta, tb, aw, ad, xa, acc_a, acc_b, s1, r1, s2, r2,
    load, send_a, recv_a, send_b, recv_b, send_1, recv_1, send_2, recv_2,
):
    row, col = lax.axis_index("row"), lax.axis_index("col")
    rx, rz, cy, core = row // SIDE, row % SIDE, col // 2, col % 2

    def at_row(off):
        return ((rx + off[0]) % SIDE) * SIDE + (rz + off[1]) % SIDE

    def at_col(slot, sign=1):
        return ((cy + sign * (slot // 2)) % SIDE) * 2 + (core + slot) % 2

    barrier = pltpu.get_barrier_semaphore()
    for slot in range(1, NCOL):
        pl.semaphore_signal(barrier, inc=1, device_id=(row, at_col(slot)), device_id_type=MESH)
    for k in range(1, NROW):
        other = at_row((k // SIDE, k % SIDE))
        pl.semaphore_signal(barrier, inc=1, device_id=(other, col), device_id_type=MESH)

    loads = [
        pltpu.make_async_copy(src, dst, load.at[i])
        for i, (src, dst) in enumerate((
            (pos_hbm, pos_v), (sup_hbm, sup_v), (bas_hbm, bas_v),
            (adj_hbm, ta.at[0, 0:32]), (prim_hbm, ta.at[0, 32:64]),
        ))
    ]
    for copy in loads:
        copy.start()
    acc_a[...] = jnp.zeros_like(acc_a)
    sel_v[...] = selectors()
    for copy in loads[:3]:
        copy.wait()
    u = pos_v[...] - SHIFT
    n = jnp.sum(u * u, axis=0, keepdims=True) + 0.5 * CORE_SQ
    uh, um, ul = split3(u)
    nh, nm, nl = split3(n)
    feats = [p.astype(f32) for p in (uh, um, ul, nh, nm, nl)]
    feats.append(jnp.ones((1, PB), f32))
    feats.append(jnp.zeros((3, PB), f32))
    sup = sup_v[...]
    bas = bas_v[...]
    bh = bas.astype(bf16).astype(f32)
    point = sup // 16
    feats += [((point % 2) * 64 + point // 2).astype(f32), (sup % 16).astype(f32), bh, bas - bh]
    ta[0, 64:96] = jnp.concatenate(feats, axis=0).astype(bf16)
    for copy in loads[3:]:
        copy.wait()

    pl.semaphore_wait(barrier, NCOL - 1 + NROW - 1)

    def copy_a(slot):
        src = 0 if slot % 2 == 0 or slot == 1 else slot - 1
        to = at_col(slot, -1) if src == 0 else at_col(1)
        return pltpu.make_async_remote_copy(
            src_ref=ta.at[src], dst_ref=ta.at[slot], send_sem=send_a.at[slot - 1], recv_sem=recv_a.at[slot - 1],
            device_id=(row, to), device_id_type=MESH,
        )

    def copy_b(k):
        off = OFFS[k]
        return pltpu.make_async_remote_copy(
            src_ref=ta.at[0], dst_ref=tb.at[k], send_sem=send_b.at[k], recv_sem=recv_b.at[k],
            device_id=(at_row((-off[0], -off[1])), col), device_id_type=MESH,
        )

    for slot in (1, 2, 6, 4):
        copy_a(slot).start()
    for k in (0, 1):
        copy_b(k).start()

    def prepare(slot):
        left = lax.dot_general(ta[slot, 0:80], sel_v[...], TN, preferred_element_type=f32)
        aw[slot] = left[:, 0:64].astype(bf16)
        ad[slot] = left[:, 64:112].astype(bf16)
        for c in range(3):
            xa[slot, c] = left[:, 128 * (c + 1) : 128 * (c + 2)]

    def pairs(right, slots, store, half=(), first=True):
        parts = right[64:80]
        rd = jnp.concatenate([parts, parts, parts], axis=0)
        accs = [None] * 4
        for i, slot in enumerate(slots):
            rw = right[0:64]
            if i in half:
                rw = rw * jnp.asarray(0.5, bf16)
            w = jnp.dot(aw[slot], rw, preferred_element_type=f32)
            d = jnp.dot(ad[slot], rd, preferred_element_type=f32)
            his, los = [], []
            for q in range(PB // CHUNK):
                rs = slice(q * CHUNK, (q + 1) * CHUNK)
                inv = lax.rsqrt(d[rs])
                s = w[rs] * inv * (inv * inv)
                for c in range(4):
                    if c < 3:
                        x = xa[slot, c, rs]
                        t = s * jnp.concatenate([x, x], axis=1)
                    else:
                        t = s
                    t = jnp.sum(t.reshape(CHUNK // 8, 8, PB), axis=0)
                    accs[c] = t if accs[c] is None else accs[c] + t
                hi = s.astype(bf16)
                his.append(hi)
                los.append((s - hi.astype(f32)).astype(bf16))
            hi, lo = jnp.concatenate(his, axis=0), jnp.concatenate(los, axis=0)
            acc_a[slot] += lax.dot_general(parts, hi, NT, preferred_element_type=f32) + lax.dot_general(
                parts, lo, NT, preferred_element_type=f32
            )
        for c in range(4):
            acc_b[store, c] = accs[c] if first else acc_b[store, c] + accs[c]

    nb = len(OFFS)
    own = ta.at[0]
    prepare(0)
    pairs(own, [0], nb, half=(0,))
    copy_a(1).wait_recv()
    prepare(1)
    pairs(own, [1], nb, half=(0,), first=False)
    for slot in (2, 6, 4):
        copy_a(slot).wait_recv()
        copy_a(slot + 1).start()
    for k in (2, 3, 4):
        copy_b(k).start()
    prepare(2)
    prepare(4)
    prepare(6)
    pairs(own, [2, 4], nb, half=(1,), first=False)
    for k in range(5, nb):
        copy_b(k).start()
    for slot in (3, 7, 5):
        copy_a(slot).wait_recv()
        prepare(slot)
    pairs(own, [3, 5], nb, half=(1,), first=False)

    def arrived(k):
        pltpu.make_async_remote_copy(
            src_ref=ta.at[0], dst_ref=tb.at[k], send_sem=send_b.at[k], recv_sem=recv_b.at[k],
            device_id=(row, at_col(1)), device_id_type=MESH,
        ).wait_recv()

    def full(k, _):
        arrived(k)
        pairs(tb.at[k], range(NCOL), k)
        return 0

    def halved(k, _):
        arrived(k)
        i = k - len(FULL)
        first = 2 * (at_row((2 * ((i + 1) % 2), 2 * ((i + 1) // 2))) < row).astype(jnp.int32)
        pairs(tb.at[k], [first + j for j in range(4)], k)
        return 0

    lax.fori_loop(0, len(FULL), full, 0)
    lax.fori_loop(len(FULL), nb, halved, 0)

    def coords(bundle):
        p = bundle[64:80].astype(f32)
        return p[0:3] + p[3:6] + p[6:9]

    def from_b(k, bundle):
        sums = [jnp.sum(acc_b[k, c], axis=0, keepdims=True) for c in range(4)]
        return jnp.concatenate(sums[:3], axis=0) - coords(bundle) * sums[3]

    def from_a(slot):
        t = acc_a[slot]
        return t[0:3] + t[3:6] + t[6:9] - coords(ta.at[slot]) * t[12:13]

    rows16 = lax.broadcasted_iota(jnp.int32, (16, PB), 0).astype(f32).astype(bf16)
    rows128 = lax.broadcasted_iota(jnp.int32, (128, PB), 0).astype(f32).astype(bf16)
    zero, unit = jnp.zeros((), bf16), jnp.ones((), bf16)

    def scatter(total, grad, bundle):
        data = bundle[80:96]
        basis = data[8:12].astype(f32) + data[12:16].astype(f32)
        lefts, rights = [], []
        for k in range(4):
            val = grad * basis[k : k + 1]
            hi = val.astype(bf16)
            lo = (val - hi.astype(f32)).astype(bf16)
            here = rows16 == data[4 + k : 5 + k]
            rights.append(
                jnp.concatenate([jnp.where(here, p[c : c + 1], zero) for p in (hi, lo) for c in range(3)], axis=0)
            )
            lefts.append(jnp.where(rows128 == data[k : k + 1], unit, zero))
        left, right = jnp.concatenate(lefts, axis=1), jnp.concatenate(rights, axis=1)
        return total + lax.dot_general(left, right, NT, preferred_element_type=f32)

    total = jnp.zeros((128, 96), f32)
    total = scatter(total, from_a(0) + from_b(nb, own), own)
    for slot in range(1, NCOL):
        total = scatter(total, from_a(slot), ta.at[slot])
    for k in range(nb):
        total = scatter(total, from_b(k, tb.at[k]), tb.at[k])
    total = jnp.concatenate([total[:, 0:48] + total[:, 48:96], jnp.zeros((128, 80), f32)], axis=1)

    s1[...] = total.reshape(2, NROW * SIDE, 128)
    sibling = pltpu.make_async_remote_copy(
        src_ref=s1.at[1 - core], dst_ref=r1, send_sem=send_1, recv_sem=recv_1,
        device_id=(row, at_col(1)), device_id_type=MESH,
    )
    sibling.start()
    sibling.wait_recv()
    both = s1[core] + r1[...]
    for j in range(NROW * SIDE):
        s2[j] = both[j : j + 1]
    for j, (dx, dy, dz) in enumerate(FAR):
        to_row, to_y = at_row((dx, dz)), (cy + dy) % SIDE
        pltpu.make_async_remote_copy(
            src_ref=s2.at[to_row * SIDE + to_y], dst_ref=r2.at[j], send_sem=send_2, recv_sem=recv_2,
            device_id=(to_row, to_y * 2 + core), device_id_type=MESH,
        ).start()
    rows = pltpu.make_async_remote_copy(
        src_ref=s2.at[0 : len(FAR)], dst_ref=r2, send_sem=send_2, recv_sem=recv_2,
        device_id=(row, at_col(1)), device_id_type=MESH,
    )
    rows.wait_recv()
    line = s2[row * SIDE + cy] + jnp.sum(r2[...], axis=0)
    out_ref[...] = jnp.concatenate([line[:, 16 * c : 16 * (c + 1)] for c in range(3)], axis=0)

    for slot in range(1, NCOL):
        copy_a(slot).wait_send()
    for k in range(nb):
        copy_b(k).wait_send()
    sibling.wait_send()
    rows.wait_send()


def shards(positions, primal, adjoint, support, basis):
    vmem = pl.BlockSpec(memory_space=pltpu.VMEM)
    hbm = pl.BlockSpec(memory_space=pltpu.HBM)
    dma = pltpu.SemaphoreType.DMA
    nb = len(OFFS)
    return pl.pallas_call(
        kernel,
        out_shape=jax.ShapeDtypeStruct((3, 16), f32),
        in_specs=[hbm] * 5,
        out_specs=vmem,
        scratch_shapes=[
            pltpu.VMEM((3, PB), f32),
            pltpu.VMEM((4, PB), jnp.int32),
            pltpu.VMEM((4, PB), f32),
            pltpu.VMEM((80, 512), bf16),
            pltpu.VMEM((NCOL, ROWS, PB), bf16),
            pltpu.VMEM((nb, ROWS, PB), bf16),
            pltpu.VMEM((NCOL, PB, 64), bf16),
            pltpu.VMEM((NCOL, PB, 48), bf16),
            pltpu.VMEM((NCOL, 3, PB, 128), f32),
            pltpu.VMEM((NCOL, 16, PB), f32),
            pltpu.VMEM((nb + 1, 4, 8, PB), f32),
            pltpu.VMEM((2, NROW * SIDE, 128), f32),
            pltpu.VMEM((NROW * SIDE, 128), f32),
            pltpu.VMEM((NROW * SIDE, 1, 128), f32),
            pltpu.VMEM((NROW * SIDE - 1, 1, 128), f32),
            dma((5,)), dma((NCOL - 1,)), dma((NCOL - 1,)), dma((nb,)), dma((nb,)),
            dma, dma, dma, dma,
        ],
        compiler_params=pltpu.CompilerParams(
            collective_id=0, has_side_effects=True, vmem_limit_bytes=60 * 2**20
        ),
    )(positions, primal.T, adjoint.T, support, basis)


def solution(mesh):
    in_specs = (
        P(None, ("row", "col")),
        P(("row", "col"), None),
        P(("row", "col"), None),
        P(None, ("row", "col")),
        P(None, ("row", "col")),
    )
    out_specs = P(None, ("row", "col"))
    return jax.shard_map(shards, mesh=mesh, in_specs=in_specs, out_specs=out_specs, check_vma=False)
```

```python
import jax
import jax.numpy as jnp
from jax import lax
from jax.experimental import pallas as pl
from jax.experimental.pallas import tpu as pltpu
from jax.sharding import PartitionSpec as P

f32, bf16 = jnp.float32, jnp.bfloat16
MESH = pl.DeviceIdType.MESH
NT = (((1,), (1,)), ((), ()))
TN = (((0,), (0,)), ((), ()))

STR, CP, CORE_SQ, SHIFT = 32, 2048, 0.01, 2.0
PB = 256
NCOL, NROW, SIDE = 8, 16, 4
FULL = ((1, 0), (0, 1), (1, 1), (3, 1), (3, 2), (2, 3))
HALF = ((2, 0), (0, 2), (2, 2))
OFFS = FULL + HALF
FAR = sorted(
    ((x, y, z) for x in range(SIDE) for y in range(SIDE) for z in range(SIDE) if x or y or z),
    key=lambda o: -sum(min(v, SIDE - v) for v in o),
)
ROWS = 96
CHUNK = 32


def selectors():
    r = lax.broadcasted_iota(jnp.int32, (80, 512), 0)
    c = lax.broadcasted_iota(jnp.int32, (80, 512), 1)
    weights = (c < 2 * STR) & (r < 2 * STR) & (r == (c + STR) % (2 * STR))
    part, slot = (c - 64) // 16, c % 16
    r3, slot3 = (r - 64) % 3, slot % 3
    distance = (c >= 64) & (c < 112)
    cross = distance & (slot < 9) & (r >= 64) & (r < 73) & ((r - 64) // 3 == part) & (r3 == slot3)
    norm = distance & (slot == 12) & (r == 73 + part)
    norm = norm | (distance & (part == 0) & (slot >= 9) & (slot < 12) & (r == 76))
    spread = (c >= 128) & (r >= 64) & (r < 73) & (r3 == (c - 128) // 128)
    return jnp.where(cross, -2.0, jnp.where(weights | norm | spread, 1.0, 0.0)).astype(bf16)


def split3(x):
    h = x.astype(bf16)
    rest = x - h.astype(f32)
    m = rest.astype(bf16)
    return h, m, (rest - m.astype(f32)).astype(bf16)


def kernel(
    pos_hbm, prim_hbm, adj_hbm, sup_hbm, bas_hbm, out_ref,
    pos_v, sup_v, bas_v, sel_v, ta, tb, aw, ad, xa, acc_a, acc_b, s1, r1, s2, r2,
    load, send_a, recv_a, send_b, recv_b, send_1, recv_1, send_2, recv_2,
):
    row, col = lax.axis_index("row"), lax.axis_index("col")
    rx, rz, cy, core = row // SIDE, row % SIDE, col // 2, col % 2

    def at_row(off):
        return ((rx + off[0]) % SIDE) * SIDE + (rz + off[1]) % SIDE

    def at_col(slot, sign=1):
        return ((cy + sign * (slot // 2)) % SIDE) * 2 + (core + slot) % 2

    barrier = pltpu.get_barrier_semaphore()
    for slot in range(1, NCOL):
        pl.semaphore_signal(barrier, inc=1, device_id=(row, at_col(slot)), device_id_type=MESH)
    for k in range(1, NROW):
        other = at_row((k // SIDE, k % SIDE))
        pl.semaphore_signal(barrier, inc=1, device_id=(other, col), device_id_type=MESH)

    loads = [
        pltpu.make_async_copy(src, dst, load.at[i])
        for i, (src, dst) in enumerate((
            (pos_hbm, pos_v), (sup_hbm, sup_v), (bas_hbm, bas_v),
            (adj_hbm, ta.at[0, 0:32]), (prim_hbm, ta.at[0, 32:64]),
        ))
    ]
    for copy in loads:
        copy.start()
    acc_a[...] = jnp.zeros_like(acc_a)
    sel_v[...] = selectors()
    for copy in loads[:3]:
        copy.wait()
    u = pos_v[...] - SHIFT
    n = jnp.sum(u * u, axis=0, keepdims=True) + 0.5 * CORE_SQ
    uh, um, ul = split3(u)
    nh, nm, nl = split3(n)
    feats = [p.astype(f32) for p in (uh, um, ul, nh, nm, nl)]
    feats.append(jnp.ones((1, PB), f32))
    feats.append(jnp.zeros((3, PB), f32))
    sup = sup_v[...]
    bas = bas_v[...]
    bh = bas.astype(bf16).astype(f32)
    point = sup // 16
    feats += [((point % 2) * 64 + point // 2).astype(f32), (sup % 16).astype(f32), bh, bas - bh]
    ta[0, 64:96] = jnp.concatenate(feats, axis=0).astype(bf16)
    for copy in loads[3:]:
        copy.wait()

    pl.semaphore_wait(barrier, NCOL - 1 + NROW - 1)

    def copy_a(slot):
        src = 0 if slot in (1, 2, 6) else slot - 1
        to = at_col(slot, -1) if src == 0 else at_col(1)
        return pltpu.make_async_remote_copy(
            src_ref=ta.at[src], dst_ref=ta.at[slot], send_sem=send_a.at[slot - 1], recv_sem=recv_a.at[slot - 1],
            device_id=(row, to), device_id_type=MESH,
        )

    def pass_on(slot):
        half, sem = (slice(0, ROWS // 2), 3) if slot == 2 else (slice(ROWS // 2, ROWS), 7)
        return pltpu.make_async_remote_copy(
            src_ref=ta.at[slot, half], dst_ref=ta.at[4, half], send_sem=send_a.at[sem], recv_sem=recv_a.at[sem],
            device_id=(row, at_col(slot, -1)), device_id_type=MESH,
        )

    def copy_b(k):
        off = OFFS[k]
        return pltpu.make_async_remote_copy(
            src_ref=ta.at[0], dst_ref=tb.at[k], send_sem=send_b.at[k], recv_sem=recv_b.at[k],
            device_id=(at_row((-off[0], -off[1])), col), device_id_type=MESH,
        )

    for slot in (1, 2, 6):
        copy_a(slot).start()
    for k in (0, 1):
        copy_b(k).start()

    def prepare(slot):
        left = lax.dot_general(ta[slot, 0:80], sel_v[...], TN, preferred_element_type=f32)
        aw[slot] = left[:, 0:64].astype(bf16)
        ad[slot] = left[:, 64:112].astype(bf16)
        for c in range(3):
            xa[slot, c] = left[:, 128 * (c + 1) : 128 * (c + 2)]

    def pairs(right, slots, store, half=(), first=True):
        parts = right[64:80]
        rd = jnp.concatenate([parts, parts, parts], axis=0)
        accs = [None] * 4
        for i, slot in enumerate(slots):
            rw = right[0:64]
            if i in half:
                rw = rw * jnp.asarray(0.5, bf16)
            w = jnp.dot(aw[slot], rw, preferred_element_type=f32)
            d = jnp.dot(ad[slot], rd, preferred_element_type=f32)
            his, los = [], []
            for q in range(PB // CHUNK):
                rs = slice(q * CHUNK, (q + 1) * CHUNK)
                inv = lax.rsqrt(d[rs])
                s = w[rs] * inv * (inv * inv)
                for c in range(4):
                    if c < 3:
                        x = xa[slot, c, rs]
                        t = s * jnp.concatenate([x, x], axis=1)
                    else:
                        t = s
                    t = jnp.sum(t.reshape(CHUNK // 8, 8, PB), axis=0)
                    accs[c] = t if accs[c] is None else accs[c] + t
                hi = s.astype(bf16)
                his.append(hi)
                los.append((s - hi.astype(f32)).astype(bf16))
            hi, lo = jnp.concatenate(his, axis=0), jnp.concatenate(los, axis=0)
            acc_a[slot] += lax.dot_general(parts, hi, NT, preferred_element_type=f32) + lax.dot_general(
                parts, lo, NT, preferred_element_type=f32
            )
        for c in range(4):
            acc_b[store, c] = accs[c] if first else acc_b[store, c] + accs[c]

    nb = len(OFFS)
    own = ta.at[0]
    prepare(0)
    pairs(own, [0], nb, half=(0,))
    copy_a(1).wait_recv()
    prepare(1)
    pairs(own, [1], nb, half=(0,), first=False)
    def arrived(k):
        pltpu.make_async_remote_copy(
            src_ref=ta.at[0], dst_ref=tb.at[k], send_sem=send_b.at[k], recv_sem=recv_b.at[k],
            device_id=(row, at_col(1)), device_id_type=MESH,
        ).wait_recv()

    def early(slots, first):
        def body(k, _):
            if first:
                arrived(k)
            pairs(tb.at[k], slots, k, first=first)
            return 0

        lax.fori_loop(0, 2, body, 0)

    for slot in (2, 6):
        copy_a(slot).wait_recv()
        pass_on(slot).start()
        copy_a(slot + 1).start()
    for k in (2, 3):
        copy_b(k).start()
    prepare(2)
    prepare(6)
    pairs(own, [2], nb, first=False)
    early([0, 1, 2, 6], True)
    for k in range(4, nb):
        copy_b(k).start()
    for slot in (3, 7):
        copy_a(slot).wait_recv()
        prepare(slot)
    pairs(own, [3], nb, first=False)
    early([3, 7], False)
    pass_on(2).wait_recv()
    pass_on(6).wait_recv()
    copy_a(5).start()
    prepare(4)
    pairs(own, [4], nb, half=(0,), first=False)
    copy_a(5).wait_recv()
    prepare(5)
    pairs(own, [5], nb, half=(0,), first=False)
    early([4, 5], False)

    def full(k, _):
        arrived(k)
        pairs(tb.at[k], range(NCOL), k)
        return 0

    def halved(k, _):
        arrived(k)
        i = k - len(FULL)
        first = 2 * (at_row((2 * ((i + 1) % 2), 2 * ((i + 1) // 2))) < row).astype(jnp.int32)
        pairs(tb.at[k], [first + j for j in range(4)], k)
        return 0

    lax.fori_loop(2, len(FULL), full, 0)
    lax.fori_loop(len(FULL), nb, halved, 0)

    def coords(bundle):
        p = bundle[64:80].astype(f32)
        return p[0:3] + p[3:6] + p[6:9]

    def from_b(k, bundle):
        sums = [jnp.sum(acc_b[k, c], axis=0, keepdims=True) for c in range(4)]
        return jnp.concatenate(sums[:3], axis=0) - coords(bundle) * sums[3]

    def from_a(slot):
        t = acc_a[slot]
        return t[0:3] + t[3:6] + t[6:9] - coords(ta.at[slot]) * t[12:13]

    rows16 = lax.broadcasted_iota(jnp.int32, (16, PB), 0).astype(f32).astype(bf16)
    rows128 = lax.broadcasted_iota(jnp.int32, (128, PB), 0).astype(f32).astype(bf16)
    zero, unit = jnp.zeros((), bf16), jnp.ones((), bf16)

    def scatter(total, grad, bundle):
        data = bundle[80:96]
        basis = data[8:12].astype(f32) + data[12:16].astype(f32)
        lefts, rights = [], []
        for k in range(4):
            val = grad * basis[k : k + 1]
            hi = val.astype(bf16)
            lo = (val - hi.astype(f32)).astype(bf16)
            here = rows16 == data[4 + k : 5 + k]
            rights.append(
                jnp.concatenate([jnp.where(here, p[c : c + 1], zero) for p in (hi, lo) for c in range(3)], axis=0)
            )
            lefts.append(jnp.where(rows128 == data[k : k + 1], unit, zero))
        left, right = jnp.concatenate(lefts, axis=1), jnp.concatenate(rights, axis=1)
        return total + lax.dot_general(left, right, NT, preferred_element_type=f32)

    total = jnp.zeros((128, 96), f32)
    total = scatter(total, from_a(0) + from_b(nb, own), own)
    for slot in range(1, NCOL):
        total = scatter(total, from_a(slot), ta.at[slot])
    for k in range(nb):
        total = scatter(total, from_b(k, tb.at[k]), tb.at[k])
    total = jnp.concatenate([total[:, 0:48] + total[:, 48:96], jnp.zeros((128, 80), f32)], axis=1)

    s1[...] = total.reshape(2, NROW * SIDE, 128)
    sibling = pltpu.make_async_remote_copy(
        src_ref=s1.at[1 - core], dst_ref=r1, send_sem=send_1, recv_sem=recv_1,
        device_id=(row, at_col(1)), device_id_type=MESH,
    )
    sibling.start()
    sibling.wait_recv()
    both = s1[core] + r1[...]
    for j in range(NROW * SIDE):
        s2[j] = both[j : j + 1]
    for j, (dx, dy, dz) in enumerate(FAR):
        to_row, to_y = at_row((dx, dz)), (cy + dy) % SIDE
        pltpu.make_async_remote_copy(
            src_ref=s2.at[to_row * SIDE + to_y], dst_ref=r2.at[j], send_sem=send_2, recv_sem=recv_2,
            device_id=(to_row, to_y * 2 + core), device_id_type=MESH,
        ).start()
    rows = pltpu.make_async_remote_copy(
        src_ref=s2.at[0 : len(FAR)], dst_ref=r2, send_sem=send_2, recv_sem=recv_2,
        device_id=(row, at_col(1)), device_id_type=MESH,
    )
    rows.wait_recv()
    line = s2[row * SIDE + cy] + jnp.sum(r2[...], axis=0)
    out_ref[...] = jnp.concatenate([line[:, 16 * c : 16 * (c + 1)] for c in range(3)], axis=0)

    for slot in (1, 2, 3, 5, 6, 7):
        copy_a(slot).wait_send()
    pass_on(2).wait_send()
    pass_on(6).wait_send()
    for k in range(nb):
        copy_b(k).wait_send()
    sibling.wait_send()
    rows.wait_send()


def shards(positions, primal, adjoint, support, basis):
    vmem = pl.BlockSpec(memory_space=pltpu.VMEM)
    hbm = pl.BlockSpec(memory_space=pltpu.HBM)
    dma = pltpu.SemaphoreType.DMA
    nb = len(OFFS)
    return pl.pallas_call(
        kernel,
        out_shape=jax.ShapeDtypeStruct((3, 16), f32),
        in_specs=[hbm] * 5,
        out_specs=vmem,
        scratch_shapes=[
            pltpu.VMEM((3, PB), f32),
            pltpu.VMEM((4, PB), jnp.int32),
            pltpu.VMEM((4, PB), f32),
            pltpu.VMEM((80, 512), bf16),
            pltpu.VMEM((NCOL, ROWS, PB), bf16),
            pltpu.VMEM((nb, ROWS, PB), bf16),
            pltpu.VMEM((NCOL, PB, 64), bf16),
            pltpu.VMEM((NCOL, PB, 48), bf16),
            pltpu.VMEM((NCOL, 3, PB, 128), f32),
            pltpu.VMEM((NCOL, 16, PB), f32),
            pltpu.VMEM((nb + 1, 4, 8, PB), f32),
            pltpu.VMEM((2, NROW * SIDE, 128), f32),
            pltpu.VMEM((NROW * SIDE, 128), f32),
            pltpu.VMEM((NROW * SIDE, 1, 128), f32),
            pltpu.VMEM((NROW * SIDE - 1, 1, 128), f32),
            dma((5,)), dma((NCOL,)), dma((NCOL,)), dma((nb,)), dma((nb,)),
            dma, dma, dma, dma,
        ],
        compiler_params=pltpu.CompilerParams(
            collective_id=0, has_side_effects=True, vmem_limit_bytes=55227 * 2**10
        ),
    )(positions, primal.T, adjoint.T, support, basis)


def solution(mesh):
    in_specs = (
        P(None, ("row", "col")),
        P(("row", "col"), None),
        P(("row", "col"), None),
        P(None, ("row", "col")),
        P(None, ("row", "col")),
    )
    out_specs = P(None, ("row", "col"))
    return jax.shard_map(shards, mesh=mesh, in_specs=in_specs, out_specs=out_specs, check_vma=False)
```

```python
import numpy as np
import jax
import jax.numpy as jnp
from jax import lax
from jax.experimental import pallas as pl
from jax.experimental.pallas import tpu as pltpu
from jax.sharding import PartitionSpec as P

f32, bf16 = jnp.float32, jnp.bfloat16
MESH = pl.DeviceIdType.MESH
NT = (((1,), (1,)), ((), ()))
TN = (((0,), (0,)), ((), ()))

STR, CP, CORE_SQ, SHIFT = 32, 2048, 0.01, 2.0
PB = 256
NCOL, NROW, SIDE = 8, 16, 4
FULL = ((1, 0), (0, 1), (1, 1), (3, 1), (3, 2), (2, 3))
HALF = ((2, 0), (0, 2), (2, 2))
OFFS = FULL + HALF
FAR = sorted(
    (o for o in np.ndindex(SIDE, SIDE, SIDE, 2) if any(o)),
    key=lambda o: -sum(min(v, SIDE - v) for v in o[:3]) - 0.5 * o[3],
)
ROWS = 96
CHUNK = 32


def selectors():
    r = lax.broadcasted_iota(jnp.int32, (80, 512), 0)
    c = lax.broadcasted_iota(jnp.int32, (80, 512), 1)
    weights = (c < 2 * STR) & (r < 2 * STR) & (r == (c + STR) % (2 * STR))
    part, slot = (c - 64) // 16, c % 16
    r3, slot3 = (r - 64) % 3, slot % 3
    distance = (c >= 64) & (c < 112)
    cross = distance & (slot < 9) & (r >= 64) & (r < 73) & ((r - 64) // 3 == part) & (r3 == slot3)
    norm = distance & (slot == 12) & (r == 73 + part)
    norm = norm | (distance & (part == 0) & (slot >= 9) & (slot < 12) & (r == 76))
    spread = (c >= 128) & (r >= 64) & (r < 73) & (r3 == (c - 128) // 128)
    return jnp.where(cross, -2.0, jnp.where(weights | norm | spread, 1.0, 0.0)).astype(bf16)


def split3(x):
    h = x.astype(bf16)
    rest = x - h.astype(f32)
    m = rest.astype(bf16)
    return h, m, (rest - m.astype(f32)).astype(bf16)


def kernel(
    pos_hbm, prim_hbm, adj_hbm, sup_hbm, bas_hbm, out_ref,
    pos_v, sup_v, bas_v, sel_v, ta, tb, aw, ad, xa, acc_a, acc_b, s1, r1,
    load, send_a, recv_a, send_b, recv_b, send_1, recv_1,
):
    row, col = lax.axis_index("row"), lax.axis_index("col")
    rx, rz, cy, core = row // SIDE, row % SIDE, col // 2, col % 2

    def at_row(off):
        return ((rx + off[0]) % SIDE) * SIDE + (rz + off[1]) % SIDE

    def at_col(slot, sign=1):
        return ((cy + sign * (slot // 2)) % SIDE) * 2 + (core + slot) % 2

    barrier = pltpu.get_barrier_semaphore()
    for slot in range(1, NCOL):
        pl.semaphore_signal(barrier, inc=1, device_id=(row, at_col(slot)), device_id_type=MESH)
    for k in range(1, NROW):
        other = at_row((k // SIDE, k % SIDE))
        pl.semaphore_signal(barrier, inc=1, device_id=(other, col), device_id_type=MESH)

    loads = [
        pltpu.make_async_copy(src, dst, load.at[i])
        for i, (src, dst) in enumerate((
            (pos_hbm, pos_v), (sup_hbm, sup_v), (bas_hbm, bas_v),
            (adj_hbm, ta.at[0, 0:32]), (prim_hbm, ta.at[0, 32:64]),
        ))
    ]
    for copy in loads:
        copy.start()
    acc_a[...] = jnp.zeros_like(acc_a)
    sel_v[...] = selectors()
    for copy in loads[:3]:
        copy.wait()
    u = pos_v[...] - SHIFT
    n = jnp.sum(u * u, axis=0, keepdims=True) + 0.5 * CORE_SQ
    uh, um, ul = split3(u)
    nh, nm, nl = split3(n)
    feats = [p.astype(f32) for p in (uh, um, ul, nh, nm, nl)]
    feats.append(jnp.ones((1, PB), f32))
    feats.append(jnp.zeros((3, PB), f32))
    sup = sup_v[...]
    bas = bas_v[...]
    bh = bas.astype(bf16).astype(f32)
    point = sup // 16
    feats += [((point % 2) * 64 + point // 2).astype(f32), (sup % 16).astype(f32), bh, bas - bh]
    ta[0, 64:96] = jnp.concatenate(feats, axis=0).astype(bf16)
    for copy in loads[3:]:
        copy.wait()

    pl.semaphore_wait(barrier, NCOL - 1 + NROW - 1)

    def copy_a(slot):
        src = 0 if slot in (1, 2, 6) else slot - 1
        to = at_col(slot, -1) if src == 0 else at_col(1)
        return pltpu.make_async_remote_copy(
            src_ref=ta.at[src], dst_ref=ta.at[slot], send_sem=send_a.at[slot - 1], recv_sem=recv_a.at[slot - 1],
            device_id=(row, to), device_id_type=MESH,
        )

    def pass_on(slot):
        half, sem = (slice(0, ROWS // 2), 3) if slot == 2 else (slice(ROWS // 2, ROWS), 7)
        return pltpu.make_async_remote_copy(
            src_ref=ta.at[slot, half], dst_ref=ta.at[4, half], send_sem=send_a.at[sem], recv_sem=recv_a.at[sem],
            device_id=(row, at_col(slot, -1)), device_id_type=MESH,
        )

    def copy_b(k):
        off = OFFS[k]
        return pltpu.make_async_remote_copy(
            src_ref=ta.at[0], dst_ref=tb.at[k], send_sem=send_b.at[k], recv_sem=recv_b.at[k],
            device_id=(at_row((-off[0], -off[1])), col), device_id_type=MESH,
        )

    for slot in (1, 2, 6):
        copy_a(slot).start()
    for k in (0, 1):
        copy_b(k).start()

    def prepare(slot):
        left = lax.dot_general(ta[slot, 0:80], sel_v[...], TN, preferred_element_type=f32)
        aw[slot] = left[:, 0:64].astype(bf16)
        ad[slot] = left[:, 64:112].astype(bf16)
        for c in range(3):
            xa[slot, c] = left[:, 128 * (c + 1) : 128 * (c + 2)]

    def pairs(right, slots, store, half=(), first=True):
        parts = right[64:80]
        rd = jnp.concatenate([parts, parts, parts], axis=0)
        accs = [None] * 4
        for i, slot in enumerate(slots):
            rw = right[0:64]
            if i in half:
                rw = rw * jnp.asarray(0.5, bf16)
            w = jnp.dot(aw[slot], rw, preferred_element_type=f32)
            d = jnp.dot(ad[slot], rd, preferred_element_type=f32)
            his, los = [], []
            for q in range(PB // CHUNK):
                rs = slice(q * CHUNK, (q + 1) * CHUNK)
                inv = lax.rsqrt(d[rs])
                s = w[rs] * inv * (inv * inv)
                for c in range(4):
                    if c < 3:
                        x = xa[slot, c, rs]
                        t = s * jnp.concatenate([x, x], axis=1)
                    else:
                        t = s
                    t = jnp.sum(t.reshape(CHUNK // 8, 8, PB), axis=0)
                    accs[c] = t if accs[c] is None else accs[c] + t
                hi = s.astype(bf16)
                his.append(hi)
                los.append((s - hi.astype(f32)).astype(bf16))
            hi, lo = jnp.concatenate(his, axis=0), jnp.concatenate(los, axis=0)
            acc_a[slot] += lax.dot_general(parts, hi, NT, preferred_element_type=f32) + lax.dot_general(
                parts, lo, NT, preferred_element_type=f32
            )
        for c in range(4):
            acc_b[store, c] = accs[c] if first else acc_b[store, c] + accs[c]

    nb = len(OFFS)
    own = ta.at[0]
    prepare(0)
    pairs(own, [0], nb, half=(0,))
    copy_a(1).wait_recv()
    prepare(1)
    pairs(own, [1], nb, half=(0,), first=False)
    def arrived(k):
        pltpu.make_async_remote_copy(
            src_ref=ta.at[0], dst_ref=tb.at[k], send_sem=send_b.at[k], recv_sem=recv_b.at[k],
            device_id=(row, at_col(1)), device_id_type=MESH,
        ).wait_recv()

    def early(slots, first):
        def body(k, _):
            if first:
                arrived(k)
            pairs(tb.at[k], slots, k, first=first)
            return 0

        lax.fori_loop(0, 2, body, 0)

    for slot in (2, 6):
        copy_a(slot).wait_recv()
        pass_on(slot).start()
        copy_a(slot + 1).start()
    for k in (2, 3):
        copy_b(k).start()
    prepare(2)
    prepare(6)
    pairs(own, [2], nb, first=False)
    early([0, 1, 2, 6], True)
    for k in range(4, nb):
        copy_b(k).start()
    for slot in (3, 7):
        copy_a(slot).wait_recv()
    pass_on(2).wait_recv()
    pass_on(6).wait_recv()
    copy_a(5).start()
    for slot in (3, 7, 4):
        prepare(slot)
    copy_a(5).wait_recv()
    prepare(5)
    pairs(own, [3, 4, 5], nb, half=(1, 2), first=False)
    early([3, 7, 4, 5], False)

    def full(k, _):
        arrived(k)
        pairs(tb.at[k], range(NCOL), k)
        return 0

    def halved(k, _):
        arrived(k)
        i = k - len(FULL)
        first = 2 * (at_row((2 * ((i + 1) % 2), 2 * ((i + 1) // 2))) < row).astype(jnp.int32)
        pairs(tb.at[k], [first + j for j in range(4)], k)
        return 0

    lax.fori_loop(2, len(FULL), full, 0)
    lax.fori_loop(len(FULL), nb, halved, 0)

    def coords(bundle):
        p = bundle[64:80].astype(f32)
        return p[0:3] + p[3:6] + p[6:9]

    def from_b(k, bundle):
        sums = [jnp.sum(acc_b[k, c], axis=0, keepdims=True) for c in range(4)]
        return jnp.concatenate(sums[:3], axis=0) - coords(bundle) * sums[3]

    def from_a(slot):
        t = acc_a[slot]
        return t[0:3] + t[3:6] + t[6:9] - coords(ta.at[slot]) * t[12:13]

    rows16 = lax.broadcasted_iota(jnp.int32, (16, PB), 0).astype(f32).astype(bf16)
    rows128 = lax.broadcasted_iota(jnp.int32, (128, PB), 0).astype(f32).astype(bf16)
    zero, unit = jnp.zeros((), bf16), jnp.ones((), bf16)

    def scatter(total, grad, bundle):
        data = bundle[80:96]
        basis = data[8:12].astype(f32) + data[12:16].astype(f32)
        lefts, rights = [], []
        for k in range(4):
            val = grad * basis[k : k + 1]
            hi = val.astype(bf16)
            lo = (val - hi.astype(f32)).astype(bf16)
            here = rows16 == data[4 + k : 5 + k]
            rights.append(
                jnp.concatenate([jnp.where(here, p[c : c + 1], zero) for p in (hi, lo) for c in range(3)], axis=0)
            )
            lefts.append(jnp.where(rows128 == data[k : k + 1], unit, zero))
        left, right = jnp.concatenate(lefts, axis=1), jnp.concatenate(rights, axis=1)
        return total + lax.dot_general(left, right, NT, preferred_element_type=f32)

    total = jnp.zeros((128, 96), f32)
    total = scatter(total, from_a(0) + from_b(nb, own), own)
    for slot in range(1, NCOL):
        total = scatter(total, from_a(slot), ta.at[slot])
    for k in range(nb):
        total = scatter(total, from_b(k, tb.at[k]), tb.at[k])
    total = jnp.concatenate([total[:, 0:48] + total[:, 48:96], jnp.zeros((128, 80), f32)], axis=1)

    for j in range(NROW * NCOL):
        s1[j] = total[j : j + 1]

    def row_of(to_row, to_y, to_core):
        return (to_core * NROW + to_row) * SIDE + to_y

    for j, (dx, dy, dz, dc) in enumerate(FAR):
        to_row, to_y, to_core = at_row((dx, dz)), (cy + dy) % SIDE, (core + dc) % 2
        pltpu.make_async_remote_copy(
            src_ref=s1.at[row_of(to_row, to_y, to_core)], dst_ref=r1.at[j], send_sem=send_1, recv_sem=recv_1,
            device_id=(to_row, to_y * 2 + to_core), device_id_type=MESH,
        ).start()
    rows = pltpu.make_async_remote_copy(
        src_ref=s1.at[0 : len(FAR)], dst_ref=r1, send_sem=send_1, recv_sem=recv_1,
        device_id=(row, at_col(1)), device_id_type=MESH,
    )
    rows.wait_recv()
    line = s1[row_of(row, cy, core)] + jnp.sum(r1[...], axis=0)
    out_ref[...] = jnp.concatenate([line[:, 16 * c : 16 * (c + 1)] for c in range(3)], axis=0)

    for slot in (1, 2, 3, 5, 6, 7):
        copy_a(slot).wait_send()
    pass_on(2).wait_send()
    pass_on(6).wait_send()
    for k in range(nb):
        copy_b(k).wait_send()
    rows.wait_send()


def shards(positions, primal, adjoint, support, basis):
    vmem = pl.BlockSpec(memory_space=pltpu.VMEM)
    hbm = pl.BlockSpec(memory_space=pltpu.HBM)
    dma = pltpu.SemaphoreType.DMA
    nb = len(OFFS)
    return pl.pallas_call(
        kernel,
        out_shape=jax.ShapeDtypeStruct((3, 16), f32),
        in_specs=[hbm] * 5,
        out_specs=vmem,
        scratch_shapes=[
            pltpu.VMEM((3, PB), f32),
            pltpu.VMEM((4, PB), jnp.int32),
            pltpu.VMEM((4, PB), f32),
            pltpu.VMEM((80, 512), bf16),
            pltpu.VMEM((NCOL, ROWS, PB), bf16),
            pltpu.VMEM((nb, ROWS, PB), bf16),
            pltpu.VMEM((NCOL, PB, 64), bf16),
            pltpu.VMEM((NCOL, PB, 48), bf16),
            pltpu.VMEM((NCOL, 3, PB, 128), f32),
            pltpu.VMEM((NCOL, 16, PB), f32),
            pltpu.VMEM((nb + 1, 4, 8, PB), f32),
            pltpu.VMEM((NROW * NCOL, 1, 128), f32),
            pltpu.VMEM((NROW * NCOL - 1, 1, 128), f32),
            dma((5,)), dma((NCOL,)), dma((NCOL,)), dma((nb,)), dma((nb,)),
            dma, dma,
        ],
        compiler_params=pltpu.CompilerParams(
            collective_id=0, has_side_effects=True, vmem_limit_bytes=55227 * 2**10
        ),
    )(positions, primal.T, adjoint.T, support, basis)


def solution(mesh):
    in_specs = (
        P(None, ("row", "col")),
        P(("row", "col"), None),
        P(("row", "col"), None),
        P(None, ("row", "col")),
        P(None, ("row", "col")),
    )
    out_specs = P(None, ("row", "col"))
    return jax.shard_map(shards, mesh=mesh, in_specs=in_specs, out_specs=out_specs, check_vma=False)
```

```python
import numpy as np
import jax
import jax.numpy as jnp
from jax import lax
from jax.experimental import pallas as pl
from jax.experimental.pallas import tpu as pltpu
from jax.sharding import PartitionSpec as P

f32, bf16 = jnp.float32, jnp.bfloat16
MESH = pl.DeviceIdType.MESH
NT = (((1,), (1,)), ((), ()))
TN = (((0,), (0,)), ((), ()))

STR, CP, CORE_SQ, SHIFT = 32, 2048, 0.01, 2.0
PB = 256
NCOL, NROW, SIDE = 8, 16, 4
FULL = ((1, 0), (0, 1), (1, 1), (3, 1), (3, 2), (2, 3))
HALF = ((2, 0), (0, 2), (2, 2))
OFFS = FULL + HALF
FAR = sorted(
    (o for o in np.ndindex(SIDE, SIDE, SIDE, 2) if any(o)),
    key=lambda o: -sum(min(v, SIDE - v) for v in o[:3]) - 0.5 * o[3],
)
ROWS = 96
CHUNK = 32


def selectors():
    r = lax.broadcasted_iota(jnp.int32, (80, 512), 0)
    c = lax.broadcasted_iota(jnp.int32, (80, 512), 1)
    weights = (c < 2 * STR) & (r < 2 * STR) & (r == (c + STR) % (2 * STR))
    part, slot = (c - 64) // 16, c % 16
    r3, slot3 = (r - 64) % 3, slot % 3
    distance = (c >= 64) & (c < 112)
    cross = distance & (slot < 9) & (r >= 64) & (r < 73) & ((r - 64) // 3 == part) & (r3 == slot3)
    norm = distance & (slot == 12) & (r == 73 + part)
    norm = norm | (distance & (part == 0) & (slot >= 9) & (slot < 12) & (r == 76))
    spread = (c >= 128) & (r >= 64) & (r < 73) & (r3 == (c - 128) // 128)
    return jnp.where(cross, -2.0, jnp.where(weights | norm | spread, 1.0, 0.0)).astype(bf16)


def split3(x):
    h = x.astype(bf16)
    rest = x - h.astype(f32)
    m = rest.astype(bf16)
    return h, m, (rest - m.astype(f32)).astype(bf16)


def kernel(
    pos_hbm, prim_hbm, adj_hbm, sup_hbm, bas_hbm, out_ref,
    pos_v, sup_v, bas_v, sel_v, ta, tb, aw, ad, xa, acc_a, acc_b, s1, r1,
    load, send_a, recv_a, send_b, recv_b, send_1, recv_1,
):
    row, col = lax.axis_index("row"), lax.axis_index("col")
    rx, rz, cy, core = row // SIDE, row % SIDE, col // 2, col % 2

    def at_row(off):
        return ((rx + off[0]) % SIDE) * SIDE + (rz + off[1]) % SIDE

    def at_col(slot, sign=1):
        return ((cy + sign * (slot // 2)) % SIDE) * 2 + (core + slot) % 2

    barrier = pltpu.get_barrier_semaphore()
    for slot in range(1, NCOL):
        pl.semaphore_signal(barrier, inc=1, device_id=(row, at_col(slot)), device_id_type=MESH)
    for k in range(1, NROW):
        other = at_row((k // SIDE, k % SIDE))
        pl.semaphore_signal(barrier, inc=1, device_id=(other, col), device_id_type=MESH)

    loads = [
        pltpu.make_async_copy(src, dst, load.at[i])
        for i, (src, dst) in enumerate((
            (pos_hbm, pos_v), (sup_hbm, sup_v), (bas_hbm, bas_v),
            (adj_hbm, ta.at[0, 0:32]), (prim_hbm, ta.at[0, 32:64]),
        ))
    ]
    for copy in loads:
        copy.start()
    acc_a[...] = jnp.zeros_like(acc_a)
    sel_v[...] = selectors()
    for copy in loads[:3]:
        copy.wait()
    u = pos_v[...] - SHIFT
    n = jnp.sum(u * u, axis=0, keepdims=True) + 0.5 * CORE_SQ
    uh, um, ul = split3(u)
    nh, nm, nl = split3(n)
    feats = [p.astype(f32) for p in (uh, um, ul, nh, nm, nl)]
    feats.append(jnp.ones((1, PB), f32))
    feats.append(jnp.zeros((3, PB), f32))
    sup = sup_v[...]
    bas = bas_v[...]
    bh = bas.astype(bf16).astype(f32)
    point = sup // 16
    feats += [((point % 2) * 64 + point // 2).astype(f32), (sup % 16).astype(f32), bh, bas - bh]
    ta[0, 64:96] = jnp.concatenate(feats, axis=0).astype(bf16)
    for copy in loads[3:]:
        copy.wait()

    pl.semaphore_wait(barrier, NCOL - 1 + NROW - 1)

    def copy_a(slot):
        src = 0 if slot in (1, 2, 6) else slot - 1
        to = at_col(slot, -1) if src == 0 else at_col(1)
        return pltpu.make_async_remote_copy(
            src_ref=ta.at[src], dst_ref=ta.at[slot], send_sem=send_a.at[slot - 1], recv_sem=recv_a.at[slot - 1],
            device_id=(row, to), device_id_type=MESH,
        )

    def pass_on(slot):
        half, sem = (slice(0, ROWS // 2), 3) if slot == 2 else (slice(ROWS // 2, ROWS), 7)
        return pltpu.make_async_remote_copy(
            src_ref=ta.at[slot, half], dst_ref=ta.at[4, half], send_sem=send_a.at[sem], recv_sem=recv_a.at[sem],
            device_id=(row, at_col(slot, -1)), device_id_type=MESH,
        )

    def copy_b(k):
        off = OFFS[k]
        return pltpu.make_async_remote_copy(
            src_ref=ta.at[0], dst_ref=tb.at[k], send_sem=send_b.at[k], recv_sem=recv_b.at[k],
            device_id=(at_row((-off[0], -off[1])), col), device_id_type=MESH,
        )

    for slot in (1, 2, 6):
        copy_a(slot).start()
    for k in (0, 1):
        copy_b(k).start()

    def prepare(slot):
        left = lax.dot_general(ta[slot, 0:80], sel_v[...], TN, preferred_element_type=f32)
        aw[slot] = left[:, 0:64].astype(bf16)
        ad[slot] = left[:, 64:112].astype(bf16)
        for c in range(3):
            xa[slot, c] = left[:, 128 * (c + 1) : 128 * (c + 2)]

    def pairs(right, slots, store, half=(), first=True):
        parts = right[64:80]
        rd = jnp.concatenate([parts, parts, parts], axis=0)
        accs = [None] * 4
        for i, slot in enumerate(slots):
            rw = right[0:64]
            if i in half:
                rw = rw * jnp.asarray(0.5, bf16)
            w = jnp.dot(aw[slot], rw, preferred_element_type=f32)
            d = jnp.dot(ad[slot], rd, preferred_element_type=f32)
            his, los = [], []
            for q in range(PB // CHUNK):
                rs = slice(q * CHUNK, (q + 1) * CHUNK)
                inv = lax.rsqrt(d[rs])
                s = w[rs] * inv * (inv * inv)
                for c in range(4):
                    if c < 3:
                        x = xa[slot, c, rs]
                        t = s * jnp.concatenate([x, x], axis=1)
                    else:
                        t = s
                    t = jnp.sum(t.reshape(CHUNK // 8, 8, PB), axis=0)
                    accs[c] = t if accs[c] is None else accs[c] + t
                hi = s.astype(bf16)
                his.append(hi)
                los.append((s - hi.astype(f32)).astype(bf16))
            hi, lo = jnp.concatenate(his, axis=0), jnp.concatenate(los, axis=0)
            acc_a[slot] += lax.dot_general(parts, hi, NT, preferred_element_type=f32) + lax.dot_general(
                parts, lo, NT, preferred_element_type=f32
            )
        for c in range(4):
            acc_b[store, c] = accs[c] if first else acc_b[store, c] + accs[c]

    nb = len(OFFS)
    own = ta.at[0]
    prepare(0)
    pairs(own, [0], nb, half=(0,))
    copy_a(1).wait_recv()
    prepare(1)
    pairs(own, [1], nb, half=(0,), first=False)
    def arrived(k):
        pltpu.make_async_remote_copy(
            src_ref=ta.at[0], dst_ref=tb.at[k], send_sem=send_b.at[k], recv_sem=recv_b.at[k],
            device_id=(row, at_col(1)), device_id_type=MESH,
        ).wait_recv()

    def early(slots, first):
        def body(k, _):
            if first:
                arrived(k)
            pairs(tb.at[k], slots, k, first=first)
            return 0

        lax.fori_loop(0, 2, body, 0)

    for slot in (2, 6):
        copy_a(slot).wait_recv()
        pass_on(slot).start()
        copy_a(slot + 1).start()
    for k in (2, 3):
        copy_b(k).start()
    prepare(2)
    prepare(6)
    pairs(own, [2], nb, first=False)
    early([0, 1, 2, 6], True)
    for k in range(4, nb):
        copy_b(k).start()
    for slot in (3, 7):
        copy_a(slot).wait_recv()
    pass_on(2).wait_recv()
    pass_on(6).wait_recv()
    copy_a(5).start()
    for slot in (3, 7, 4):
        prepare(slot)
    copy_a(5).wait_recv()
    prepare(5)
    pairs(own, [3, 4, 5], nb, half=(1, 2), first=False)
    early([3, 7, 4, 5], False)

    def full(k, _):
        for j in range(2):
            arrived(2 * k + j)
        for j in range(2):
            pairs(tb.at[2 * k + j], range(NCOL), 2 * k + j)
        return 0

    def halved(k, _):
        arrived(k)
        i = k - len(FULL)
        first = 2 * (at_row((2 * ((i + 1) % 2), 2 * ((i + 1) // 2))) < row).astype(jnp.int32)
        pairs(tb.at[k], [first + j for j in range(4)], k)
        return 0

    lax.fori_loop(1, len(FULL) // 2, full, 0)
    lax.fori_loop(len(FULL), nb, halved, 0)

    def coords(bundle):
        p = bundle[64:80].astype(f32)
        return p[0:3] + p[3:6] + p[6:9]

    def from_b(k, bundle):
        sums = [jnp.sum(acc_b[k, c], axis=0, keepdims=True) for c in range(4)]
        return jnp.concatenate(sums[:3], axis=0) - coords(bundle) * sums[3]

    def from_a(slot):
        t = acc_a[slot]
        return t[0:3] + t[3:6] + t[6:9] - coords(ta.at[slot]) * t[12:13]

    rows16 = lax.broadcasted_iota(jnp.int32, (16, PB), 0).astype(f32).astype(bf16)
    rows128 = lax.broadcasted_iota(jnp.int32, (128, PB), 0).astype(f32).astype(bf16)
    zero, unit = jnp.zeros((), bf16), jnp.ones((), bf16)

    def scatter(total, grad, bundle):
        data = bundle[80:96]
        basis = data[8:12].astype(f32) + data[12:16].astype(f32)
        lefts, rights = [], []
        for k in range(4):
            val = grad * basis[k : k + 1]
            hi = val.astype(bf16)
            lo = (val - hi.astype(f32)).astype(bf16)
            here = rows16 == data[4 + k : 5 + k]
            rights.append(
                jnp.concatenate([jnp.where(here, p[c : c + 1], zero) for p in (hi, lo) for c in range(3)], axis=0)
            )
            lefts.append(jnp.where(rows128 == data[k : k + 1], unit, zero))
        left, right = jnp.concatenate(lefts, axis=1), jnp.concatenate(rights, axis=1)
        return total + lax.dot_general(left, right, NT, preferred_element_type=f32)

    total = jnp.zeros((128, 96), f32)
    total = scatter(total, from_a(0) + from_b(nb, own), own)
    for slot in range(1, NCOL):
        total = scatter(total, from_a(slot), ta.at[slot])
    for k in range(nb):
        total = scatter(total, from_b(k, tb.at[k]), tb.at[k])
    total = jnp.concatenate([total[:, 0:48] + total[:, 48:96], jnp.zeros((128, 80), f32)], axis=1)

    s1[...] = total.reshape(NROW * NCOL, 1, 128)

    def row_of(to_row, to_y, to_core):
        return (to_core * NROW + to_row) * SIDE + to_y

    for j, (dx, dy, dz, dc) in enumerate(FAR):
        to_row, to_y, to_core = at_row((dx, dz)), (cy + dy) % SIDE, (core + dc) % 2
        pltpu.make_async_remote_copy(
            src_ref=s1.at[row_of(to_row, to_y, to_core)], dst_ref=r1.at[j], send_sem=send_1, recv_sem=recv_1,
            device_id=(to_row, to_y * 2 + to_core), device_id_type=MESH,
        ).start()
    rows = pltpu.make_async_remote_copy(
        src_ref=s1.at[0 : len(FAR)], dst_ref=r1, send_sem=send_1, recv_sem=recv_1,
        device_id=(row, at_col(1)), device_id_type=MESH,
    )
    rows.wait_recv()
    line = s1[row_of(row, cy, core)] + jnp.sum(r1[...], axis=0)
    out_ref[...] = jnp.concatenate([line[:, 16 * c : 16 * (c + 1)] for c in range(3)], axis=0)

    for slot in (1, 2, 3, 5, 6, 7):
        copy_a(slot).wait_send()
    pass_on(2).wait_send()
    pass_on(6).wait_send()
    for k in range(nb):
        copy_b(k).wait_send()
    rows.wait_send()


def shards(positions, primal, adjoint, support, basis):
    vmem = pl.BlockSpec(memory_space=pltpu.VMEM)
    hbm = pl.BlockSpec(memory_space=pltpu.HBM)
    dma = pltpu.SemaphoreType.DMA
    nb = len(OFFS)
    return pl.pallas_call(
        kernel,
        out_shape=jax.ShapeDtypeStruct((3, 16), f32),
        in_specs=[hbm] * 5,
        out_specs=vmem,
        scratch_shapes=[
            pltpu.VMEM((3, PB), f32),
            pltpu.VMEM((4, PB), jnp.int32),
            pltpu.VMEM((4, PB), f32),
            pltpu.VMEM((80, 512), bf16),
            pltpu.VMEM((NCOL, ROWS, PB), bf16),
            pltpu.VMEM((nb, ROWS, PB), bf16),
            pltpu.VMEM((NCOL, PB, 64), bf16),
            pltpu.VMEM((NCOL, PB, 48), bf16),
            pltpu.VMEM((NCOL, 3, PB, 128), f32),
            pltpu.VMEM((NCOL, 16, PB), f32),
            pltpu.VMEM((nb + 1, 4, 8, PB), f32),
            pltpu.VMEM((NROW * NCOL, 1, 128), f32),
            pltpu.VMEM((NROW * NCOL - 1, 1, 128), f32),
            dma((5,)), dma((NCOL,)), dma((NCOL,)), dma((nb,)), dma((nb,)),
            dma, dma,
        ],
        compiler_params=pltpu.CompilerParams(
            collective_id=0, has_side_effects=True, vmem_limit_bytes=55227 * 2**10
        ),
    )(positions, primal.T, adjoint.T, support, basis)


def solution(mesh):
    in_specs = (
        P(None, ("row", "col")),
        P(("row", "col"), None),
        P(("row", "col"), None),
        P(None, ("row", "col")),
        P(None, ("row", "col")),
    )
    out_specs = P(None, ("row", "col"))
    return jax.shard_map(shards, mesh=mesh, in_specs=in_specs, out_specs=out_specs, check_vma=False)
```

```python
import numpy as np
import jax
import jax.numpy as jnp
from jax import lax
from jax.experimental import pallas as pl
from jax.experimental.pallas import tpu as pltpu
from jax.sharding import PartitionSpec as P

f32, bf16 = jnp.float32, jnp.bfloat16
MESH = pl.DeviceIdType.MESH
NT = (((1,), (1,)), ((), ()))
TN = (((0,), (0,)), ((), ()))

STR, CP, CORE_SQ, SHIFT = 32, 2048, 0.01, 2.0
PB = 256
NCOL, NROW, SIDE = 8, 16, 4
FULL = ((1, 0), (0, 1), (1, 1), (3, 1), (3, 2), (2, 3))
HALF = ((2, 0), (0, 2), (2, 2))
OFFS = FULL + HALF
FAR = sorted(
    (o for o in np.ndindex(SIDE, SIDE, SIDE, 2) if any(o)),
    key=lambda o: -sum(min(v, SIDE - v) for v in o[:3]) - 0.5 * o[3],
)
ROWS = 96
CHUNK = 32


def selectors():
    r = lax.broadcasted_iota(jnp.int32, (80, 512), 0)
    c = lax.broadcasted_iota(jnp.int32, (80, 512), 1)
    weights = (c < 2 * STR) & (r < 2 * STR) & (r == (c + STR) % (2 * STR))
    part, slot = (c - 64) // 16, c % 16
    r3, slot3 = (r - 64) % 3, slot % 3
    distance = (c >= 64) & (c < 112)
    cross = distance & (slot < 9) & (r >= 64) & (r < 73) & ((r - 64) // 3 == part) & (r3 == slot3)
    norm = distance & (slot == 12) & (r == 73 + part)
    norm = norm | (distance & (part == 0) & (slot >= 9) & (slot < 12) & (r == 76))
    spread = (c >= 128) & (r >= 64) & (r < 73) & (r3 == (c - 128) // 128)
    return jnp.where(cross, -2.0, jnp.where(weights | norm | spread, 1.0, 0.0)).astype(bf16)


def split3(x):
    h = x.astype(bf16)
    rest = x - h.astype(f32)
    m = rest.astype(bf16)
    return h, m, (rest - m.astype(f32)).astype(bf16)


def kernel(
    pos_hbm, prim_hbm, adj_hbm, sup_hbm, bas_hbm, out_ref,
    pos_v, sup_v, bas_v, sel_v, ta, tb, aw, ad, xa, acc_a, acc_b, s1, r1,
    load, send_a, recv_a, send_b, recv_b, send_1, recv_1,
):
    row, col = lax.axis_index("row"), lax.axis_index("col")
    rx, rz, cy, core = row // SIDE, row % SIDE, col // 2, col % 2

    def at_row(off):
        return ((rx + off[0]) % SIDE) * SIDE + (rz + off[1]) % SIDE

    def at_col(slot, sign=1):
        return ((cy + sign * (slot // 2)) % SIDE) * 2 + (core + slot) % 2

    loads = [
        pltpu.make_async_copy(src, dst, load.at[i])
        for i, (src, dst) in enumerate((
            (pos_hbm, pos_v), (sup_hbm, sup_v), (bas_hbm, bas_v),
            (adj_hbm, ta.at[0, 0:32]), (prim_hbm, ta.at[0, 32:64]),
        ))
    ]
    for copy in loads:
        copy.start()
    barrier = pltpu.get_barrier_semaphore()
    for slot in range(1, NCOL):
        pl.semaphore_signal(barrier, inc=1, device_id=(row, at_col(slot)), device_id_type=MESH)
    for k in sorted(range(1, NROW), key=lambda k: sum(min(v, SIDE - v) for v in divmod(k, SIDE))):
        other = at_row((k // SIDE, k % SIDE))
        pl.semaphore_signal(barrier, inc=1, device_id=(other, col), device_id_type=MESH)

    acc_a[...] = jnp.zeros_like(acc_a)
    sel_v[...] = selectors()
    for copy in loads[:3]:
        copy.wait()
    u = pos_v[...] - SHIFT
    n = jnp.sum(u * u, axis=0, keepdims=True) + 0.5 * CORE_SQ
    uh, um, ul = split3(u)
    nh, nm, nl = split3(n)
    feats = [p.astype(f32) for p in (uh, um, ul, nh, nm, nl)]
    feats.append(jnp.ones((1, PB), f32))
    feats.append(jnp.zeros((3, PB), f32))
    sup = sup_v[...]
    bas = bas_v[...]
    bh = bas.astype(bf16).astype(f32)
    point = sup // 16
    feats += [((point % 2) * 64 + point // 2).astype(f32), (sup % 16).astype(f32), bh, bas - bh]
    ta[0, 64:96] = jnp.concatenate(feats, axis=0).astype(bf16)
    for copy in loads[3:]:
        copy.wait()

    pl.semaphore_wait(barrier, NCOL - 1 + NROW - 1)

    def copy_a(slot):
        src = 0 if slot in (1, 2, 6) else slot - 1
        to = at_col(slot, -1) if src == 0 else at_col(1)
        return pltpu.make_async_remote_copy(
            src_ref=ta.at[src], dst_ref=ta.at[slot], send_sem=send_a.at[slot - 1], recv_sem=recv_a.at[slot - 1],
            device_id=(row, to), device_id_type=MESH,
        )

    def pass_on(slot):
        half, sem = (slice(0, ROWS // 2), 3) if slot == 2 else (slice(ROWS // 2, ROWS), 7)
        return pltpu.make_async_remote_copy(
            src_ref=ta.at[slot, half], dst_ref=ta.at[4, half], send_sem=send_a.at[sem], recv_sem=recv_a.at[sem],
            device_id=(row, at_col(slot, -1)), device_id_type=MESH,
        )

    def copy_b(k):
        off = OFFS[k]
        return pltpu.make_async_remote_copy(
            src_ref=ta.at[0], dst_ref=tb.at[k], send_sem=send_b.at[k], recv_sem=recv_b.at[k],
            device_id=(at_row((-off[0], -off[1])), col), device_id_type=MESH,
        )

    for slot in (1, 2, 6):
        copy_a(slot).start()
    for k in (0, 1):
        copy_b(k).start()

    def prepare(slot):
        left = lax.dot_general(ta[slot, 0:80], sel_v[...], TN, preferred_element_type=f32)
        aw[slot] = left[:, 0:64].astype(bf16)
        ad[slot] = left[:, 64:112].astype(bf16)
        for c in range(3):
            xa[slot, c] = left[:, 128 * (c + 1) : 128 * (c + 2)]

    def pairs(right, slots, store, half=(), first=True):
        parts = right[64:80]
        rd = jnp.concatenate([parts, parts, parts], axis=0)
        accs = [None] * 4
        for i, slot in enumerate(slots):
            rw = right[0:64]
            if i in half:
                rw = rw * jnp.asarray(0.5, bf16)
            w = jnp.dot(aw[slot], rw, preferred_element_type=f32)
            d = jnp.dot(ad[slot], rd, preferred_element_type=f32)
            his, los = [], []
            for q in range(PB // CHUNK):
                rs = slice(q * CHUNK, (q + 1) * CHUNK)
                inv = lax.rsqrt(d[rs])
                s = w[rs] * inv * (inv * inv)
                for c in range(4):
                    if c < 3:
                        x = xa[slot, c, rs]
                        t = s * jnp.concatenate([x, x], axis=1)
                    else:
                        t = s
                    t = jnp.sum(t.reshape(CHUNK // 8, 8, PB), axis=0)
                    accs[c] = t if accs[c] is None else accs[c] + t
                hi = s.astype(bf16)
                his.append(hi)
                los.append((s - hi.astype(f32)).astype(bf16))
            hi, lo = jnp.concatenate(his, axis=0), jnp.concatenate(los, axis=0)
            acc_a[slot] += lax.dot_general(parts, hi, NT, preferred_element_type=f32) + lax.dot_general(
                parts, lo, NT, preferred_element_type=f32
            )
        for c in range(4):
            acc_b[store, c] = accs[c] if first else acc_b[store, c] + accs[c]

    nb = len(OFFS)
    own = ta.at[0]
    prepare(0)
    pairs(own, [0], nb, half=(0,))
    copy_a(1).wait_recv()
    prepare(1)
    pairs(own, [1], nb, half=(0,), first=False)
    def arrived(k):
        pltpu.make_async_remote_copy(
            src_ref=ta.at[0], dst_ref=tb.at[k], send_sem=send_b.at[k], recv_sem=recv_b.at[k],
            device_id=(row, at_col(1)), device_id_type=MESH,
        ).wait_recv()

    def early(slots, first):
        def body(k, _):
            if first:
                arrived(k)
            pairs(tb.at[k], slots, k, first=first)
            return 0

        lax.fori_loop(0, 2, body, 0)

    for slot in (2, 6):
        copy_a(slot).wait_recv()
        pass_on(slot).start()
        copy_a(slot + 1).start()
    for k in (2, 3):
        copy_b(k).start()
    prepare(2)
    prepare(6)
    early([0, 1, 2, 6], True)
    for k in range(4, nb):
        copy_b(k).start()
    for slot in (3, 7):
        copy_a(slot).wait_recv()
    pass_on(2).wait_recv()
    pass_on(6).wait_recv()
    copy_a(5).start()
    for slot in (3, 7, 4):
        prepare(slot)
    copy_a(5).wait_recv()
    prepare(5)
    pairs(own, [2, 3, 4, 5], nb, half=(2, 3), first=False)
    early([3, 7, 4, 5], False)

    def full(k, _):
        for j in range(2):
            arrived(2 * k + j)
        for j in range(2):
            pairs(tb.at[2 * k + j], range(NCOL), 2 * k + j)
        return 0

    def halved(k, _):
        arrived(k)
        i = k - len(FULL)
        first = 2 * (at_row((2 * ((i + 1) % 2), 2 * ((i + 1) // 2))) < row).astype(jnp.int32)
        pairs(tb.at[k], [first + j for j in range(4)], k)
        return 0

    lax.fori_loop(1, len(FULL) // 2, full, 0)
    lax.fori_loop(len(FULL), nb, halved, 0)

    def coords(bundle):
        p = bundle[64:80].astype(f32)
        return p[0:3] + p[3:6] + p[6:9]

    def from_b(k, bundle):
        sums = [jnp.sum(acc_b[k, c], axis=0, keepdims=True) for c in range(4)]
        return jnp.concatenate(sums[:3], axis=0) - coords(bundle) * sums[3]

    def from_a(slot):
        t = acc_a[slot]
        return t[0:3] + t[3:6] + t[6:9] - coords(ta.at[slot]) * t[12:13]

    rows16 = lax.broadcasted_iota(jnp.int32, (16, PB), 0).astype(f32).astype(bf16)
    rows128 = lax.broadcasted_iota(jnp.int32, (128, PB), 0).astype(f32).astype(bf16)
    zero, unit = jnp.zeros((), bf16), jnp.ones((), bf16)

    def scatter(total, grad, bundle):
        data = bundle[80:96]
        basis = data[8:12].astype(f32) + data[12:16].astype(f32)
        lefts, rights = [], []
        for k in range(4):
            val = grad * basis[k : k + 1]
            hi = val.astype(bf16)
            lo = (val - hi.astype(f32)).astype(bf16)
            here = rows16 == data[4 + k : 5 + k]
            rights.append(
                jnp.concatenate([jnp.where(here, p[c : c + 1], zero) for p in (hi, lo) for c in range(3)], axis=0)
            )
            lefts.append(jnp.where(rows128 == data[k : k + 1], unit, zero))
        left, right = jnp.concatenate(lefts, axis=1), jnp.concatenate(rights, axis=1)
        return total + lax.dot_general(left, right, NT, preferred_element_type=f32)

    total = jnp.zeros((128, 96), f32)
    total = scatter(total, from_a(0) + from_b(nb, own), own)
    for slot in range(1, NCOL):
        total = scatter(total, from_a(slot), ta.at[slot])
    for k in range(nb):
        total = scatter(total, from_b(k, tb.at[k]), tb.at[k])
    total = jnp.concatenate([total[:, 0:48] + total[:, 48:96], jnp.zeros((128, 80), f32)], axis=1)

    s1[...] = total.reshape(NROW * NCOL, 1, 128)

    def row_of(to_row, to_y, to_core):
        return (to_core * NROW + to_row) * SIDE + to_y

    for j, (dx, dy, dz, dc) in enumerate(FAR):
        to_row, to_y, to_core = at_row((dx, dz)), (cy + dy) % SIDE, (core + dc) % 2
        pltpu.make_async_remote_copy(
            src_ref=s1.at[row_of(to_row, to_y, to_core)], dst_ref=r1.at[j], send_sem=send_1, recv_sem=recv_1,
            device_id=(to_row, to_y * 2 + to_core), device_id_type=MESH,
        ).start()
    rows = pltpu.make_async_remote_copy(
        src_ref=s1.at[0 : len(FAR)], dst_ref=r1, send_sem=send_1, recv_sem=recv_1,
        device_id=(row, at_col(1)), device_id_type=MESH,
    )
    rows.wait_recv()
    line = s1[row_of(row, cy, core)] + jnp.sum(r1[...], axis=0)
    out_ref[...] = jnp.concatenate([line[:, 16 * c : 16 * (c + 1)] for c in range(3)], axis=0)

    for slot in (1, 2, 3, 5, 6, 7):
        copy_a(slot).wait_send()
    pass_on(2).wait_send()
    pass_on(6).wait_send()
    for k in range(nb):
        copy_b(k).wait_send()
    rows.wait_send()


def shards(positions, primal, adjoint, support, basis):
    vmem = pl.BlockSpec(memory_space=pltpu.VMEM)
    hbm = pl.BlockSpec(memory_space=pltpu.HBM)
    dma = pltpu.SemaphoreType.DMA
    nb = len(OFFS)
    return pl.pallas_call(
        kernel,
        out_shape=jax.ShapeDtypeStruct((3, 16), f32),
        in_specs=[hbm] * 5,
        out_specs=vmem,
        scratch_shapes=[
            pltpu.VMEM((3, PB), f32),
            pltpu.VMEM((4, PB), jnp.int32),
            pltpu.VMEM((4, PB), f32),
            pltpu.VMEM((80, 512), bf16),
            pltpu.VMEM((NCOL, ROWS, PB), bf16),
            pltpu.VMEM((nb, ROWS, PB), bf16),
            pltpu.VMEM((NCOL, PB, 64), bf16),
            pltpu.VMEM((NCOL, PB, 48), bf16),
            pltpu.VMEM((NCOL, 3, PB, 128), f32),
            pltpu.VMEM((NCOL, 16, PB), f32),
            pltpu.VMEM((nb + 1, 4, 8, PB), f32),
            pltpu.VMEM((NROW * NCOL, 1, 128), f32),
            pltpu.VMEM((NROW * NCOL - 1, 1, 128), f32),
            dma((5,)), dma((NCOL,)), dma((NCOL,)), dma((nb,)), dma((nb,)),
            dma, dma,
        ],
        compiler_params=pltpu.CompilerParams(
            collective_id=0, has_side_effects=True, vmem_limit_bytes=55227 * 2**10
        ),
    )(positions, primal.T, adjoint.T, support, basis)


def solution(mesh):
    in_specs = (
        P(None, ("row", "col")),
        P(("row", "col"), None),
        P(("row", "col"), None),
        P(None, ("row", "col")),
        P(None, ("row", "col")),
    )
    out_specs = P(None, ("row", "col"))
    return jax.shard_map(shards, mesh=mesh, in_specs=in_specs, out_specs=out_specs, check_vma=False)
```

```python
import numpy as np
import jax
import jax.numpy as jnp
from jax import lax
from jax.experimental import pallas as pl
from jax.experimental.pallas import tpu as pltpu
from jax.sharding import PartitionSpec as P

f32, bf16 = jnp.float32, jnp.bfloat16
MESH = pl.DeviceIdType.MESH
NT = (((1,), (1,)), ((), ()))
TN = (((0,), (0,)), ((), ()))

STR, CP, CORE_SQ, SHIFT = 32, 2048, 0.01, 2.0
PB = 256
NCOL, NROW, SIDE = 8, 16, 4
FULL = ((1, 0), (0, 1), (1, 1), (3, 1), (3, 2), (2, 3))
HALF = ((2, 0), (0, 2), (2, 2))
OFFS = FULL + HALF
FAR = sorted(
    (o for o in np.ndindex(SIDE, SIDE, SIDE, 2) if any(o)),
    key=lambda o: -sum(min(v, SIDE - v) for v in o[:3]) - 0.5 * o[3],
)
ROWS = 96
CHUNK = 32


def selectors():
    r = lax.broadcasted_iota(jnp.int32, (80, 512), 0)
    c = lax.broadcasted_iota(jnp.int32, (80, 512), 1)
    weights = (c < 2 * STR) & (r < 2 * STR) & (r == (c + STR) % (2 * STR))
    part, slot = (c - 64) // 16, c % 16
    r3, slot3 = (r - 64) % 3, slot % 3
    distance = (c >= 64) & (c < 112)
    cross = distance & (slot < 9) & (r >= 64) & (r < 73) & ((r - 64) // 3 == part) & (r3 == slot3)
    norm = distance & (slot == 12) & (r == 73 + part)
    norm = norm | (distance & (part == 0) & (slot >= 9) & (slot < 12) & (r == 76))
    spread = (c >= 128) & (r >= 64) & (r < 73) & (r3 == (c - 128) // 128)
    return jnp.where(cross, -2.0, jnp.where(weights | norm | spread, 1.0, 0.0)).astype(bf16)


def split3(x):
    h = x.astype(bf16)
    rest = x - h.astype(f32)
    m = rest.astype(bf16)
    return h, m, (rest - m.astype(f32)).astype(bf16)


def kernel(
    pos_hbm, prim_hbm, adj_hbm, sup_hbm, bas_hbm, out_ref,
    pos_v, sup_v, bas_v, sel_v, ta, tb, aw, ad, xa, acc_a, acc_b, s1, r1,
    load, send_a, recv_a, send_b, recv_b, send_1, recv_1,
):
    row, col = lax.axis_index("row"), lax.axis_index("col")
    rx, rz, cy, core = row // SIDE, row % SIDE, col // 2, col % 2

    def at_row(off):
        return ((rx + off[0]) % SIDE) * SIDE + (rz + off[1]) % SIDE

    def at_col(slot, sign=1):
        return ((cy + sign * (slot // 2)) % SIDE) * 2 + (core + slot) % 2

    loads = [
        pltpu.make_async_copy(src, dst, load.at[i])
        for i, (src, dst) in enumerate((
            (pos_hbm, pos_v), (sup_hbm, sup_v), (bas_hbm, bas_v),
            (adj_hbm, ta.at[0, 0:32]), (prim_hbm, ta.at[0, 32:64]),
        ))
    ]
    for copy in loads:
        copy.start()
    barrier = pltpu.get_barrier_semaphore()
    for slot in range(1, NCOL):
        pl.semaphore_signal(barrier, inc=1, device_id=(row, at_col(slot)), device_id_type=MESH)
    for k in sorted(range(1, NROW), key=lambda k: sum(min(v, SIDE - v) for v in divmod(k, SIDE))):
        other = at_row((k // SIDE, k % SIDE))
        pl.semaphore_signal(barrier, inc=1, device_id=(other, col), device_id_type=MESH)

    acc_a[...] = jnp.zeros_like(acc_a)
    sel_v[...] = selectors()
    for copy in loads[:3]:
        copy.wait()
    u = pos_v[...] - SHIFT
    n = jnp.sum(u * u, axis=0, keepdims=True) + 0.5 * CORE_SQ
    uh, um, ul = split3(u)
    nh, nm, nl = split3(n)
    feats = [p.astype(f32) for p in (uh, um, ul, nh, nm, nl)]
    feats.append(jnp.ones((1, PB), f32))
    feats.append(jnp.zeros((3, PB), f32))
    sup = sup_v[...]
    bas = bas_v[...]
    bh = bas.astype(bf16).astype(f32)
    point = sup // 16
    feats += [((point % 2) * 64 + point // 2).astype(f32), (sup % 16).astype(f32), bh, bas - bh]
    ta[0, 64:96] = jnp.concatenate(feats, axis=0).astype(bf16)
    for copy in loads[3:]:
        copy.wait()

    pl.semaphore_wait(barrier, NCOL - 1 + NROW - 1)

    def copy_a(slot):
        src = 0 if slot in (1, 2, 6) else slot - 1
        to = at_col(slot, -1) if src == 0 else at_col(1)
        return pltpu.make_async_remote_copy(
            src_ref=ta.at[src], dst_ref=ta.at[slot], send_sem=send_a.at[slot - 1], recv_sem=recv_a.at[slot - 1],
            device_id=(row, to), device_id_type=MESH,
        )

    def pass_on(slot):
        half, sem = (slice(0, ROWS // 2), 3) if slot == 2 else (slice(ROWS // 2, ROWS), 7)
        return pltpu.make_async_remote_copy(
            src_ref=ta.at[slot, half], dst_ref=ta.at[4, half], send_sem=send_a.at[sem], recv_sem=recv_a.at[sem],
            device_id=(row, at_col(slot, -1)), device_id_type=MESH,
        )

    def copy_b(k):
        off = OFFS[k]
        return pltpu.make_async_remote_copy(
            src_ref=ta.at[0], dst_ref=tb.at[k], send_sem=send_b.at[k], recv_sem=recv_b.at[k],
            device_id=(at_row((-off[0], -off[1])), col), device_id_type=MESH,
        )

    for slot in (1, 2, 6):
        copy_a(slot).start()
    for k in (0, 1):
        copy_b(k).start()

    def prepare(slot):
        left = lax.dot_general(ta[slot, 0:80], sel_v[...], TN, preferred_element_type=f32)
        aw[slot] = left[:, 0:64].astype(bf16)
        ad[slot] = left[:, 64:112].astype(bf16)
        for c in range(3):
            xa[slot, c] = left[:, 128 * (c + 1) : 128 * (c + 2)]

    def pairs(right, slots, store, half=(), first=True):
        parts = right[64:80]
        rd = jnp.concatenate([parts, parts, parts], axis=0)
        accs = [None] * 4
        for i, slot in enumerate(slots):
            rw = right[0:64]
            if i in half:
                rw = rw * jnp.asarray(0.5, bf16)
            w = jnp.dot(aw[slot], rw, preferred_element_type=f32)
            d = jnp.dot(ad[slot], rd, preferred_element_type=f32)
            his, los = [], []
            for q in range(PB // CHUNK):
                rs = slice(q * CHUNK, (q + 1) * CHUNK)
                inv = lax.rsqrt(d[rs])
                s = w[rs] * inv * (inv * inv)
                for c in range(4):
                    if c < 3:
                        x = xa[slot, c, rs]
                        t = s * jnp.concatenate([x, x], axis=1)
                    else:
                        t = s
                    t = jnp.sum(t.reshape(CHUNK // 8, 8, PB), axis=0)
                    accs[c] = t if accs[c] is None else accs[c] + t
                hi = s.astype(bf16)
                his.append(hi)
                los.append((s - hi.astype(f32)).astype(bf16))
            hi, lo = jnp.concatenate(his, axis=0), jnp.concatenate(los, axis=0)
            acc_a[slot] += lax.dot_general(parts, hi, NT, preferred_element_type=f32) + lax.dot_general(
                parts, lo, NT, preferred_element_type=f32
            )
        for c in range(4):
            acc_b[store, c] = accs[c] if first else acc_b[store, c] + accs[c]

    nb = len(OFFS)
    own = ta.at[0]
    prepare(0)
    pairs(own, [0], nb, half=(0,))
    copy_a(1).wait_recv()
    prepare(1)
    pairs(own, [1], nb, half=(0,), first=False)
    def arrived(k):
        pltpu.make_async_remote_copy(
            src_ref=ta.at[0], dst_ref=tb.at[k], send_sem=send_b.at[k], recv_sem=recv_b.at[k],
            device_id=(row, at_col(1)), device_id_type=MESH,
        ).wait_recv()

    def early(slots, first):
        def body(k, _):
            if first:
                arrived(k)
            pairs(tb.at[k], slots, k, first=first)
            return 0

        lax.fori_loop(0, 2, body, 0)

    for slot in (2, 6):
        copy_a(slot).wait_recv()
        pass_on(slot).start()
        copy_a(slot + 1).start()
    for k in (2, 3):
        copy_b(k).start()
    prepare(2)
    prepare(6)
    early([0, 1, 2, 6], True)
    for k in range(4, nb):
        copy_b(k).start()
    for slot in (3, 7):
        copy_a(slot).wait_recv()
    pass_on(2).wait_recv()
    pass_on(6).wait_recv()
    copy_a(5).start()
    for slot in (3, 7, 4):
        prepare(slot)
    copy_a(5).wait_recv()
    prepare(5)
    pairs(own, [2, 3, 4, 5], nb, half=(2, 3), first=False)
    early([3, 7, 4, 5], False)

    def full(k, _):
        for j in range(2):
            arrived(2 * k + j)
        for j in range(2):
            pairs(tb.at[2 * k + j], range(NCOL), 2 * k + j)
        return 0

    def halved(k, _):
        arrived(k)
        i = k - len(FULL)
        first = 2 * (at_row((2 * ((i + 1) % 2), 2 * ((i + 1) // 2))) < row).astype(jnp.int32)
        pairs(tb.at[k], [first + j for j in range(4)], k)
        return 0

    lax.fori_loop(1, len(FULL) // 2, full, 0)
    lax.fori_loop(len(FULL), nb, halved, 0)

    def coords(bundle):
        p = bundle[64:80].astype(f32)
        return p[0:3] + p[3:6] + p[6:9]

    def from_b(k, bundle):
        sums = [jnp.sum(acc_b[k, c], axis=0, keepdims=True) for c in range(4)]
        return jnp.concatenate(sums[:3], axis=0) - coords(bundle) * sums[3]

    def from_a(slot):
        t = acc_a[slot]
        return t[0:3] + t[3:6] + t[6:9] - coords(ta.at[slot]) * t[12:13]

    rows16 = lax.broadcasted_iota(jnp.int32, (16, PB), 0).astype(f32).astype(bf16)
    rows128 = lax.broadcasted_iota(jnp.int32, (128, PB), 0).astype(f32).astype(bf16)
    zero, unit = jnp.zeros((), bf16), jnp.ones((), bf16)

    def scatter(total, grad, bundle):
        data = bundle[80:96]
        basis = data[8:12].astype(f32) + data[12:16].astype(f32)
        lefts, rights = [], []
        for k in range(4):
            val = grad * basis[k : k + 1]
            hi = val.astype(bf16)
            lo = (val - hi.astype(f32)).astype(bf16)
            here = rows16 == data[4 + k : 5 + k]
            rights.append(
                jnp.concatenate([jnp.where(here, p[c : c + 1], zero) for p in (hi, lo) for c in range(3)], axis=0)
            )
            lefts.append(jnp.where(rows128 == data[k : k + 1], unit, zero))
        left, right = jnp.concatenate(lefts, axis=1), jnp.concatenate(rights, axis=1)
        return total + lax.dot_general(left, right, NT, preferred_element_type=f32)

    total = jnp.zeros((128, 96), f32)
    total = scatter(total, from_a(0) + from_b(nb, own), own)
    for slot in range(1, NCOL):
        total = scatter(total, from_a(slot), ta.at[slot])
    for k in range(nb):
        total = scatter(total, from_b(k, tb.at[k]), tb.at[k])
    total = jnp.concatenate([total[:, 0:48] + total[:, 48:96], jnp.zeros((128, 80), f32)], axis=1)

    s1[...] = total.reshape(NROW * NCOL, 1, 128)

    def row_of(to_row, to_y, to_core):
        return (to_core * NROW + to_row) * SIDE + to_y

    xs, ys, zs = ([(p + d) % SIDE for d in range(SIDE)] for p in (rx, cy, rz))
    cores = [core, 1 - core]
    for j, (dx, dy, dz, dc) in enumerate(FAR):
        to_row, to_y, to_core = xs[dx] * SIDE + zs[dz], ys[dy], cores[dc]
        pltpu.make_async_remote_copy(
            src_ref=s1.at[row_of(to_row, to_y, to_core)], dst_ref=r1.at[j], send_sem=send_1, recv_sem=recv_1,
            device_id=(to_row, to_y * 2 + to_core), device_id_type=MESH,
        ).start()
    rows = pltpu.make_async_remote_copy(
        src_ref=s1.at[0 : len(FAR)], dst_ref=r1, send_sem=send_1, recv_sem=recv_1,
        device_id=(row, at_col(1)), device_id_type=MESH,
    )
    rows.wait_recv()
    line = s1[row_of(row, cy, core)] + jnp.sum(r1[...], axis=0)
    out_ref[...] = jnp.concatenate([line[:, 16 * c : 16 * (c + 1)] for c in range(3)], axis=0)

    for slot in (1, 2, 3, 5, 6, 7):
        copy_a(slot).wait_send()
    pass_on(2).wait_send()
    pass_on(6).wait_send()
    for k in range(nb):
        copy_b(k).wait_send()
    rows.wait_send()


def shards(positions, primal, adjoint, support, basis):
    vmem = pl.BlockSpec(memory_space=pltpu.VMEM)
    hbm = pl.BlockSpec(memory_space=pltpu.HBM)
    dma = pltpu.SemaphoreType.DMA
    nb = len(OFFS)
    return pl.pallas_call(
        kernel,
        out_shape=jax.ShapeDtypeStruct((3, 16), f32),
        in_specs=[hbm] * 5,
        out_specs=vmem,
        scratch_shapes=[
            pltpu.VMEM((3, PB), f32),
            pltpu.VMEM((4, PB), jnp.int32),
            pltpu.VMEM((4, PB), f32),
            pltpu.VMEM((80, 512), bf16),
            pltpu.VMEM((NCOL, ROWS, PB), bf16),
            pltpu.VMEM((nb, ROWS, PB), bf16),
            pltpu.VMEM((NCOL, PB, 64), bf16),
            pltpu.VMEM((NCOL, PB, 48), bf16),
            pltpu.VMEM((NCOL, 3, PB, 128), f32),
            pltpu.VMEM((NCOL, 16, PB), f32),
            pltpu.VMEM((nb + 1, 4, 8, PB), f32),
            pltpu.VMEM((NROW * NCOL, 1, 128), f32),
            pltpu.VMEM((NROW * NCOL - 1, 1, 128), f32),
            dma((5,)), dma((NCOL,)), dma((NCOL,)), dma((nb,)), dma((nb,)),
            dma, dma,
        ],
        compiler_params=pltpu.CompilerParams(
            collective_id=0, has_side_effects=True, vmem_limit_bytes=55227 * 2**10
        ),
    )(positions, primal.T, adjoint.T, support, basis)


def solution(mesh):
    in_specs = (
        P(None, ("row", "col")),
        P(("row", "col"), None),
        P(("row", "col"), None),
        P(None, ("row", "col")),
        P(None, ("row", "col")),
    )
    out_specs = P(None, ("row", "col"))
    return jax.shard_map(shards, mesh=mesh, in_specs=in_specs, out_specs=out_specs, check_vma=False)
```
